32 devices in a mesh: ctx: 8 (over y, x, core), ch: 4 (over z).
Axes of the slice: x: 2, y: 2, z: 4, core: 2. Of those that a mesh axis runs over, the one named last changes fastest.
Arguments:
- proj: bfloat16 [3, 4096, 2048], P(None, 'ch', 'ctx'), may hold values from -6 to 6
- short_filter: float32 [3, 4096, 3], P(None, 'ch'), may hold values from -3 to 3
- residues: float32 [4096, 16], P('ch'), may hold values from -1.8 to 1.8
- decays: float32 [4096, 16], P('ch'), may hold values from 0.00024414062 to 0.03
- skip: float32 [4096], P('ch'), may hold values from -1 to 1
- w_out: bfloat16 [4096, 4096], P(None, 'ch'), may hold values from -0.09375 to 0.09375
Outputs:
- mixed_out: bfloat16 [2048, 4096], P('ctx', 'ch')
The draws below stay inside these ranges and needn't reach their ends.
All inputs are finite; a program needn't handle non-finite values.
Results may differ from the reference program's by a relative error of at most 0.015.
Values may be sent and summed in bfloat16 or wider, within the bound.
A program may use at most 192 MiB of HBM per device.

```python
import math
import jax
import jax.numpy as jnp
from jax import lax

D = 4096
MODES = 16
SEQ = 2048


def shard_levels(key, dims, pieces, smallest, high):
    level = 1.0
    for axis_at, blocks in pieces:
        heights = jax.random.uniform(jax.random.fold_in(jax.random.fold_in(key, 6), axis_at), (blocks,), jnp.float32, smallest / len(pieces), high / len(pieces))
        level = level * jnp.repeat(jnp.exp(heights), dims[axis_at] // blocks).reshape((-1,) + (1,) * (len(dims) - 1 - axis_at))
    return level


def scatter_about(rng, shape, scale, limit, split=(), kind=jnp.bfloat16):
    factor_of = shard_levels(rng, shape, split, -0.22, 0.18) if split else 1.0
    drawn = jax.random.normal(rng, shape, jnp.float32) * scale * factor_of
    return jnp.minimum(jnp.maximum(drawn, -limit), limit).astype(kind)


def setup_inputs(seed: int = 0) -> dict:
    arg_keys = jax.random.split(jax.random.key(seed), 7)
    return {
        "proj": scatter_about(arg_keys[0], (3, D, SEQ), 1.0, 6.0, ((1, 4), (2, 8))),
        "short_filter": scatter_about(arg_keys[1], (3, D, 3), 0.6, 3.0, ((1, 4),), jnp.float32),
        "residues": scatter_about(arg_keys[2], (D, MODES), 0.3, 1.8, ((0, 4),), jnp.float32),
        "decays": jnp.clip(jnp.exp(math.log(0.03) - 4.8112082 * jax.random.uniform(arg_keys[3], (D, MODES), jnp.float32) ** shard_levels(arg_keys[3], (D, MODES), ((0, 4),), -0.2, 0.2)), 0.00024414062, 0.03),
        "skip": jnp.clip(jax.random.uniform(arg_keys[4], (D,), jnp.float32, -1.0, 1.0) * shard_levels(arg_keys[4], (D,), ((0, 4),), -0.4, 0.0), -1.0, 1.0),
        "w_out": scatter_about(arg_keys[5], (D, D), D ** -0.5, 0.09375, ((1, 4),)),
    }


def filter_taps(mode_gain, mode_rate, length):
    positions = jnp.arange(length, dtype=jnp.int32).astype(jnp.float32)

    def add_mode(mode, running):
        one_gain = lax.dynamic_slice_in_dim(mode_gain, mode, 1, 1)
        one_rate = lax.dynamic_slice_in_dim(mode_rate, mode, 1, 1)
        return running + one_gain * jnp.exp(-one_rate * positions[None, :])
    initial = jnp.zeros((mode_gain.shape[0], length), jnp.float32)
    return lax.fori_loop(0, mode_gain.shape[1], add_mode, initial)

def reference(proj, short_filter, residues, decays, skip, w_out):
    inputs = proj.astype(jnp.float32)
    padded = jnp.pad(inputs, ((0, 0), (0, 0), (2, 0)))
    shortmix = short_filter[:, :, 0:1] * inputs + short_filter[:, :, 1:2] * padded[:, :, 1:-1] + short_filter[:, :, 2:3] * padded[:, :, :-2]
    query = shortmix[0].astype(jnp.bfloat16)
    signal = (shortmix[1] * shortmix[2]).astype(jnp.bfloat16)
    mode_gain = residues * jnp.sqrt(-jnp.expm1(-2.0 * decays))
    width, length = signal.shape
    block = math.gcd(width, 256)
    count = width // block
    extent = 2 * length

    def one_block(operands):
        signal_block, gain_block, rate_block = operands
        taps = filter_taps(gain_block, rate_block, length)
        spectrum = jnp.fft.rfft(signal_block.astype(jnp.float32), n=extent, axis=1) * jnp.fft.rfft(taps, n=extent, axis=1)
        return jnp.fft.irfft(spectrum, n=extent, axis=1)[:, :length].astype(jnp.float32)
    longconv = lax.map(one_block, (signal.reshape(count, block, length), mode_gain.reshape(count, block, MODES), decays.reshape(count, block, MODES)))
    longconv = longconv.reshape(width, length)
    longconv = lax.optimization_barrier(longconv.astype(jnp.bfloat16)).astype(jnp.float32)
    gated = (query.astype(jnp.float32) * (longconv + skip[:, None] * signal.astype(jnp.float32))).astype(jnp.bfloat16)
    return jnp.dot(gated.T, w_out, preferred_element_type=jnp.float32).astype(jnp.bfloat16)
```

```python
import functools

import jax
import jax.numpy as jnp
from jax import lax
from jax.experimental import pallas as pl
from jax.experimental.pallas import tpu as pltpu
from jax.sharding import PartitionSpec as P

MESH = pl.DeviceIdType.MESH
LANES = 128


def rounded(value):
    return value.astype(jnp.bfloat16).astype(jnp.float32)


def fused_kernel(
    dims, proj_hbm, coef_ref, w_hbm, out_ref,
    proj_v, w_v, mixed, signal, gate_rows, states, gathered, total,
    in_sem, halo_send, halo_recv, state_send, state_recv, send_sem, recv_sem,
):
    n_ctx, n_ch, length, groups, modes, halo, parts = dims
    width = groups * LANES
    rows = length // parts
    ctx = lax.axis_index("ctx")
    ch = lax.axis_index("ch")

    load_proj = pltpu.make_async_copy(proj_hbm, proj_v, in_sem.at[0])
    load_proj.start()
    load_w = pltpu.make_async_copy(w_hbm, w_v, in_sem.at[1])
    load_w.start()

    barrier = pltpu.get_barrier_semaphore()

    def greet(step, carry):
        pl.semaphore_signal(
            barrier, inc=1, device_id={"ctx": lax.rem(ctx + step, n_ctx)}, device_id_type=MESH
        )
        return carry

    lax.fori_loop(1, n_ctx, greet, 0)

    @pl.when(ch > 0)
    def _():
        pl.semaphore_signal(barrier, inc=1, device_id={"ch": ch - 1}, device_id_type=MESH)

    @pl.when(ch < n_ch - 1)
    def _():
        pl.semaphore_signal(barrier, inc=1, device_id={"ch": ch + 1}, device_id_type=MESH)

    inner = jnp.where(ch > 0, 1, 0) + jnp.where(ch < n_ch - 1, 1, 0)

    def coef(index):
        return coef_ref[index * groups:(index + 1) * groups, :]

    decay = [coef(m) for m in range(modes)]
    taps = [[coef(4 * modes + 3 * i + m) for m in range(3)] for i in range(3)]
    skip = coef(4 * modes + 9)

    load_proj.wait()
    row_ids = lax.broadcasted_iota(jnp.int32, (length, length), 0)
    col_ids = lax.broadcasted_iota(jnp.int32, (length, length), 1)
    eye = jnp.where(row_ids == col_ids, 1.0, 0.0).astype(jnp.bfloat16)
    wide = min(width, 256)
    for i in range(3):
        for part in range(width // wide):
            turned = lax.dot_general(
                eye, proj_v[i, part * wide:(part + 1) * wide, :],
                (((1,), (1,)), ((), ())), preferred_element_type=jnp.float32,
            )
            for j in range(wide // LANES):
                group = part * (wide // LANES) + j
                mixed[i, pl.ds(halo * groups + group, length, stride=groups), :] = (
                    turned[:, j * LANES:(j + 1) * LANES]
                )

    pl.semaphore_wait(barrier, n_ctx - 1 + inner)

    edge = halo * groups
    halo_copy = pltpu.make_async_remote_copy(
        src_ref=mixed.at[:, pl.ds(length * groups, edge), :],
        dst_ref=mixed.at[:, pl.ds(0, edge), :],
        send_sem=halo_send.at[0],
        recv_sem=halo_recv.at[0],
        device_id={"ctx": lax.rem(ctx + 1, n_ctx)},
        device_id_type=MESH,
    )

    @pl.when(ctx < n_ctx - 1)
    def _():
        halo_copy.start()

    @pl.when(ctx == 0)
    def _():
        mixed[:, pl.ds(0, edge), :] = jnp.zeros((3, edge, LANES), jnp.float32)

    def short(i, t):
        def at(back):
            start = (t + halo - back) * groups
            if not isinstance(start, int):
                start = pl.multiple_of(start, groups)
            return mixed[i, pl.ds(start, groups), :]

        return taps[i][0] * at(0) + taps[i][1] * at(1) + taps[i][2] * at(2)

    def row_of(t):
        start = t * groups
        if not isinstance(start, int):
            start = pl.multiple_of(start, groups)
        return pl.ds(start, groups)

    def absorb(t, state):
        value = rounded(short(1, t) * short(2, t))
        signal[row_of(t), :] = value
        return tuple(d * s + value for d, s in zip(decay, state))

    empty = tuple(jnp.zeros((groups, LANES), jnp.float32) for _ in range(modes))
    state = lax.fori_loop(2, length, absorb, empty, unroll=2)

    @pl.when(ctx > 0)
    def _():
        halo_copy.wait_recv()

    first = rounded(short(1, 0) * short(2, 0))
    second = rounded(short(1, 1) * short(2, 1))
    signal[row_of(0), :] = first
    signal[row_of(1), :] = second
    for m in range(modes):
        own = state[m] + coef(3 * modes + m) * (decay[m] * first + second)
        states[ctx, m * groups:(m + 1) * groups, :] = own

    def state_copy(source, target):
        return pltpu.make_async_remote_copy(
            src_ref=states.at[source],
            dst_ref=states.at[source],
            send_sem=state_send.at[target],
            recv_sem=state_recv.at[source],
            device_id={"ctx": target},
            device_id_type=MESH,
        )

    def send_state(target, carry):
        state_copy(ctx, target).start()
        return carry

    lax.fori_loop(ctx + 1, n_ctx, send_state, 0)

    def take_state(source, carried):
        state_copy(source, ctx).wait_recv()
        return tuple(
            coef(2 * modes + m) * carried[m] + states[source, m * groups:(m + 1) * groups, :]
            for m in range(modes)
        )

    state = lax.fori_loop(0, ctx, take_state, empty)

    gain = [coef(modes + m) for m in range(modes)]

    def advance(t, state):
        value = signal[row_of(t), :]
        state = tuple(d * s + value for d, s in zip(decay, state))
        terms = [g * s for g, s in zip(gain, state)]
        while len(terms) > 1:
            terms = [sum(terms[k:k + 2][1:], terms[k]) for k in range(0, len(terms), 2)]
        gate_rows[row_of(t), :] = rounded(short(0, t)) * (rounded(terms[0]) + skip * value)
        return state

    def block_copy(block, part, side):
        window = gathered.at[block, pl.ds(pl.multiple_of(part * rows, rows), rows), :]
        return pltpu.make_async_remote_copy(
            src_ref=window,
            dst_ref=window,
            send_sem=send_sem.at[side, block, part],
            recv_sem=recv_sem.at[block, part],
            device_id={"ch": jnp.clip(ch - 1 + 2 * side, 0, n_ch - 1)},
            device_id_type=MESH,
        )

    for part in range(parts):
        state = lax.fori_loop(part * rows, (part + 1) * rows, advance, state, unroll=2)
        for group in range(groups):
            tile = gate_rows[pl.ds(part * rows * groups + group, rows, stride=groups), :]
            gathered[ch, part * rows:(part + 1) * rows, group * LANES:(group + 1) * LANES] = (
                tile.astype(jnp.bfloat16)
            )

        @pl.when(ch > 0)
        def _():
            block_copy(ch, part, 0).start()

        @pl.when(ch < n_ch - 1)
        def _():
            block_copy(ch, part, 1).start()

    load_w.wait()

    def product(block, part):
        lhs = gathered[block, pl.ds(pl.multiple_of(part * rows, rows), rows), :]
        rhs = w_v[pl.ds(pl.multiple_of(block * width, width), width), :]
        return jnp.dot(lhs, rhs, preferred_element_type=jnp.float32)

    def own_part(part, carry):
        total[pl.ds(pl.multiple_of(part * rows, rows), rows), :] = product(ch, part)
        return carry

    lax.fori_loop(0, parts, own_part, 0)

    for distance in range(1, n_ch):
        def one_part(part, carry):
            for side in (0, 1):
                block = ch + distance if side == 0 else ch - distance
                here = block < n_ch if side == 0 else block >= 0
                further = (ch > 0) if side == 0 else (ch < n_ch - 1)

                @pl.when(here)
                def _():
                    block_copy(block, part, side).wait_recv()

                @pl.when(here & further)
                def _():
                    block_copy(block, part, side).start()

                @pl.when(here)
                def _():
                    total[pl.ds(pl.multiple_of(part * rows, rows), rows), :] += product(
                        block, part
                    )
            return carry

        lax.fori_loop(0, parts, one_part, 0)

    out_ref[...] = total[...].astype(jnp.bfloat16)

    @pl.when(ctx < n_ctx - 1)
    def _():
        halo_copy.wait_send()

    def sent_state(target, carry):
        state_copy(ctx, target).wait_send()
        return carry

    lax.fori_loop(ctx + 1, n_ctx, sent_state, 0)

    def sent_left(block, carry):
        for part in range(parts):
            block_copy(block, part, 0).wait_send()
        return carry

    def sent_right(block, carry):
        for part in range(parts):
            block_copy(block, part, 1).wait_send()
        return carry

    @pl.when(ch > 0)
    def _():
        lax.fori_loop(ch, n_ch, sent_left, 0)

    @pl.when(ch < n_ch - 1)
    def _():
        lax.fori_loop(0, ch + 1, sent_right, 0)


def per_device(dims_mesh, proj, short_filter, residues, decays, skip, w_out):
    n_ctx, n_ch = dims_mesh
    _, width, length = proj.shape
    modes = residues.shape[1]
    groups = width // LANES
    halo = max(2, 8 // groups)
    parts = 4
    rate = decays.T
    coefs = jnp.concatenate(
        [
            jnp.exp(-rate),
            residues.T * jnp.sqrt(-jnp.expm1(-2.0 * rate)),
            jnp.exp(-float(length) * rate),
            jnp.exp(-float(length - 2) * rate),
            short_filter.transpose(0, 2, 1).reshape(9, width),
            skip[None, :],
        ],
        axis=0,
    )
    count = coefs.shape[0]
    coefs = coefs.reshape(count * groups, LANES)
    dims = (n_ctx, n_ch, length, groups, modes, halo, parts)
    features = w_out.shape[1]
    total_width = w_out.shape[0]
    return pl.pallas_call(
        functools.partial(fused_kernel, dims),
        out_shape=jax.ShapeDtypeStruct((length, features), jnp.bfloat16),
        in_specs=[
            pl.BlockSpec(memory_space=pl.ANY),
            pl.BlockSpec(memory_space=pltpu.VMEM),
            pl.BlockSpec(memory_space=pl.ANY),
        ],
        out_specs=pl.BlockSpec(memory_space=pltpu.VMEM),
        scratch_shapes=[
            pltpu.VMEM(proj.shape, jnp.bfloat16),
            pltpu.VMEM(w_out.shape, jnp.bfloat16),
            pltpu.VMEM((3, (length + halo) * groups, LANES), jnp.float32),
            pltpu.VMEM((length * groups, LANES), jnp.float32),
            pltpu.VMEM((length * groups, LANES), jnp.float32),
            pltpu.VMEM((n_ctx, modes * groups, LANES), jnp.float32),
            pltpu.VMEM((n_ch, length, width), jnp.bfloat16),
            pltpu.VMEM((length, features), jnp.float32),
            pltpu.SemaphoreType.DMA((2,)),
            pltpu.SemaphoreType.DMA((1,)),
            pltpu.SemaphoreType.DMA((1,)),
            pltpu.SemaphoreType.DMA((n_ctx,)),
            pltpu.SemaphoreType.DMA((n_ctx,)),
            pltpu.SemaphoreType.DMA((2, n_ch, parts)),
            pltpu.SemaphoreType.DMA((n_ch, parts)),
        ],
        compiler_params=pltpu.CompilerParams(
            collective_id=0, has_side_effects=True, vmem_limit_bytes=48 * 1024 * 1024
        ),
        cost_estimate=pl.CostEstimate(
            flops=2 * length * total_width * features,
            bytes_accessed=2 * (total_width * features + 3 * width * length + length * features),
            transcendentals=0,
        ),
    )(proj, coefs, w_out)


def solution(mesh):
    in_specs = (
        P(None, "ch", "ctx"),
        P(None, "ch", None),
        P("ch", None),
        P("ch", None),
        P("ch"),
        P(None, "ch"),
    )
    dims_mesh = (mesh.shape["ctx"], mesh.shape["ch"])
    return jax.shard_map(
        functools.partial(per_device, dims_mesh),
        mesh=mesh, in_specs=in_specs, out_specs=P("ctx", "ch"), check_vma=False,
    )
```

```python
import functools

import jax
import jax.numpy as jnp
from jax import lax
from jax.experimental import pallas as pl
from jax.experimental.pallas import tpu as pltpu
from jax.sharding import PartitionSpec as P

MESH = pl.DeviceIdType.MESH
LANES = 128


def rounded(value):
    return value.astype(jnp.bfloat16).astype(jnp.float32)


def fused_kernel(
    dims, proj_hbm, short_hbm, weight_hbm, rate_hbm, skip_hbm, w_hbm, out_ref,
    proj_v, short_v, weight_v, rate_v, skip_v, coef_ref, w_v, mixed, signal, gate_rows, states, gathered, total,
    in_sem, halo_send, halo_recv, state_send, state_recv, send_sem, recv_sem,
):
    n_ctx, n_ch, length, groups, modes, halo, parts = dims
    width = groups * LANES
    rows = length // parts
    ctx = lax.axis_index("ctx")
    ch = lax.axis_index("ch")

    small = [
        pltpu.make_async_copy(source, target, in_sem.at[2 + k])
        for k, (source, target) in enumerate(
            [(rate_hbm, rate_v), (weight_hbm, weight_v), (short_hbm, short_v), (skip_hbm, skip_v)]
        )
    ]
    for copy in small:
        copy.start()
    load_proj = pltpu.make_async_copy(proj_hbm, proj_v, in_sem.at[0])
    load_proj.start()
    load_w = pltpu.make_async_copy(w_hbm, w_v, in_sem.at[1])
    load_w.start()

    barrier = pltpu.get_barrier_semaphore()

    def greet(step, carry):
        pl.semaphore_signal(
            barrier, inc=1, device_id={"ctx": lax.rem(ctx + step, n_ctx)}, device_id_type=MESH
        )
        return carry

    lax.fori_loop(1, n_ctx, greet, 0)

    @pl.when(ch > 0)
    def _():
        pl.semaphore_signal(barrier, inc=1, device_id={"ch": ch - 1}, device_id_type=MESH)

    @pl.when(ch < n_ch - 1)
    def _():
        pl.semaphore_signal(barrier, inc=1, device_id={"ch": ch + 1}, device_id_type=MESH)

    inner = jnp.where(ch > 0, 1, 0) + jnp.where(ch < n_ch - 1, 1, 0)

    for copy in small:
        copy.wait()

    def spread(base, value):
        for group in range(groups):
            coef_ref[pl.ds(base * groups + group, value.shape[0], stride=groups), :] = (
                value[:, group * LANES:(group + 1) * LANES]
            )

    rate = rate_v[...]
    spread(0, jnp.exp(-rate))
    spread(modes, weight_v[...] * jnp.sqrt(jnp.tanh(rate) * (1.0 + jnp.exp(-2.0 * rate))))
    spread(2 * modes, jnp.exp(-float(length) * rate))
    spread(3 * modes, jnp.exp(-float(length - 2) * rate))
    for i in range(3):
        spread(4 * modes + 3 * i, short_v[i])
    spread(4 * modes + 9, skip_v[...])

    def coef(index):
        return coef_ref[index * groups:(index + 1) * groups, :]

    decay = [coef(m) for m in range(modes)]
    taps = [[coef(4 * modes + 3 * i + m) for m in range(3)] for i in range(3)]
    skip = coef(4 * modes + 9)

    load_proj.wait()
    row_ids = lax.broadcasted_iota(jnp.int32, (length, length), 0)
    col_ids = lax.broadcasted_iota(jnp.int32, (length, length), 1)
    eye = jnp.where(row_ids == col_ids, 1.0, 0.0).astype(jnp.bfloat16)
    wide = min(width, 256)
    for i in range(3):
        for part in range(width // wide):
            turned = lax.dot_general(
                eye, proj_v[i, part * wide:(part + 1) * wide, :],
                (((1,), (1,)), ((), ())), preferred_element_type=jnp.float32,
            )
            for j in range(wide // LANES):
                group = part * (wide // LANES) + j
                mixed[i, pl.ds(halo * groups + group, length, stride=groups), :] = (
                    turned[:, j * LANES:(j + 1) * LANES]
                )

    pl.semaphore_wait(barrier, n_ctx - 1 + inner)

    edge = halo * groups
    halo_copy = pltpu.make_async_remote_copy(
        src_ref=mixed.at[:, pl.ds(length * groups, edge), :],
        dst_ref=mixed.at[:, pl.ds(0, edge), :],
        send_sem=halo_send.at[0],
        recv_sem=halo_recv.at[0],
        device_id={"ctx": lax.rem(ctx + 1, n_ctx)},
        device_id_type=MESH,
    )

    @pl.when(ctx < n_ctx - 1)
    def _():
        halo_copy.start()

    @pl.when(ctx == 0)
    def _():
        mixed[:, pl.ds(0, edge), :] = jnp.zeros((3, edge, LANES), jnp.float32)

    def short(i, t):
        def at(back):
            start = (t + halo - back) * groups
            if not isinstance(start, int):
                start = pl.multiple_of(start, groups)
            return mixed[i, pl.ds(start, groups), :]

        return taps[i][0] * at(0) + taps[i][1] * at(1) + taps[i][2] * at(2)

    def row_of(t):
        start = t * groups
        if not isinstance(start, int):
            start = pl.multiple_of(start, groups)
        return pl.ds(start, groups)

    def absorb(t, state):
        value = rounded(short(1, t) * short(2, t))
        signal[row_of(t), :] = value
        return tuple(d * s + value for d, s in zip(decay, state))

    empty = tuple(jnp.zeros((groups, LANES), jnp.float32) for _ in range(modes))
    state = lax.fori_loop(2, length, absorb, empty, unroll=2)

    @pl.when(ctx > 0)
    def _():
        halo_copy.wait_recv()

    first = rounded(short(1, 0) * short(2, 0))
    second = rounded(short(1, 1) * short(2, 1))
    signal[row_of(0), :] = first
    signal[row_of(1), :] = second
    for m in range(modes):
        own = state[m] + coef(3 * modes + m) * (decay[m] * first + second)
        states[ctx, m * groups:(m + 1) * groups, :] = own

    def state_copy(source, target):
        return pltpu.make_async_remote_copy(
            src_ref=states.at[source],
            dst_ref=states.at[source],
            send_sem=state_send.at[target],
            recv_sem=state_recv.at[source],
            device_id={"ctx": target},
            device_id_type=MESH,
        )

    def send_state(target, carry):
        state_copy(ctx, target).start()
        return carry

    lax.fori_loop(ctx + 1, n_ctx, send_state, 0)

    def take_state(source, carried):
        state_copy(source, ctx).wait_recv()
        return tuple(
            coef(2 * modes + m) * carried[m] + states[source, m * groups:(m + 1) * groups, :]
            for m in range(modes)
        )

    state = lax.fori_loop(0, ctx, take_state, empty)

    gain = [coef(modes + m) for m in range(modes)]

    def advance(t, state):
        value = signal[row_of(t), :]
        state = tuple(d * s + value for d, s in zip(decay, state))
        terms = [g * s for g, s in zip(gain, state)]
        while len(terms) > 1:
            terms = [sum(terms[k:k + 2][1:], terms[k]) for k in range(0, len(terms), 2)]
        gate_rows[row_of(t), :] = rounded(short(0, t)) * (rounded(terms[0]) + skip * value)
        return state

    def block_copy(block, part, side):
        window = gathered.at[block, pl.ds(pl.multiple_of(part * rows, rows), rows), :]
        return pltpu.make_async_remote_copy(
            src_ref=window,
            dst_ref=window,
            send_sem=send_sem.at[side, block, part],
            recv_sem=recv_sem.at[block, part],
            device_id={"ch": jnp.clip(ch - 1 + 2 * side, 0, n_ch - 1)},
            device_id_type=MESH,
        )

    for part in range(parts):
        state = lax.fori_loop(part * rows, (part + 1) * rows, advance, state, unroll=2)
        for group in range(groups):
            tile = gate_rows[pl.ds(part * rows * groups + group, rows, stride=groups), :]
            gathered[ch, part * rows:(part + 1) * rows, group * LANES:(group + 1) * LANES] = (
                tile.astype(jnp.bfloat16)
            )

        @pl.when(ch > 0)
        def _():
            block_copy(ch, part, 0).start()

        @pl.when(ch < n_ch - 1)
        def _():
            block_copy(ch, part, 1).start()

    load_w.wait()

    def product(block, part):
        lhs = gathered[block, pl.ds(pl.multiple_of(part * rows, rows), rows), :]
        rhs = w_v[pl.ds(pl.multiple_of(block * width, width), width), :]
        return jnp.dot(lhs, rhs, preferred_element_type=jnp.float32)

    def own_part(part, carry):
        total[pl.ds(pl.multiple_of(part * rows, rows), rows), :] = product(ch, part)
        return carry

    lax.fori_loop(0, parts, own_part, 0)

    for distance in range(1, n_ch):
        def one_part(part, carry):
            for side in (0, 1):
                block = ch + distance if side == 0 else ch - distance
                here = block < n_ch if side == 0 else block >= 0
                further = (ch > 0) if side == 0 else (ch < n_ch - 1)

                @pl.when(here)
                def _():
                    block_copy(block, part, side).wait_recv()

                @pl.when(here & further)
                def _():
                    block_copy(block, part, side).start()

                @pl.when(here)
                def _():
                    total[pl.ds(pl.multiple_of(part * rows, rows), rows), :] += product(
                        block, part
                    )
            return carry

        lax.fori_loop(0, parts, one_part, 0)

    out_ref[...] = total[...].astype(jnp.bfloat16)

    @pl.when(ctx < n_ctx - 1)
    def _():
        halo_copy.wait_send()

    def sent_state(target, carry):
        state_copy(ctx, target).wait_send()
        return carry

    lax.fori_loop(ctx + 1, n_ctx, sent_state, 0)

    def sent_left(block, carry):
        for part in range(parts):
            block_copy(block, part, 0).wait_send()
        return carry

    def sent_right(block, carry):
        for part in range(parts):
            block_copy(block, part, 1).wait_send()
        return carry

    @pl.when(ch > 0)
    def _():
        lax.fori_loop(ch, n_ch, sent_left, 0)

    @pl.when(ch < n_ch - 1)
    def _():
        lax.fori_loop(0, ch + 1, sent_right, 0)


def per_device(dims_mesh, proj, short_filter, residues, decays, skip, w_out):
    n_ctx, n_ch = dims_mesh
    _, width, length = proj.shape
    modes = residues.shape[1]
    groups = width // LANES
    halo = max(2, 8 // groups)
    parts = 4
    dims = (n_ctx, n_ch, length, groups, modes, halo, parts)
    features = w_out.shape[1]
    total_width = w_out.shape[0]
    return pl.pallas_call(
        functools.partial(fused_kernel, dims),
        out_shape=jax.ShapeDtypeStruct((length, features), jnp.bfloat16),
        in_specs=[
            pl.BlockSpec(memory_space=pl.ANY),
        ] * 6,
        out_specs=pl.BlockSpec(memory_space=pltpu.VMEM),
        scratch_shapes=[
            pltpu.VMEM(proj.shape, jnp.bfloat16),
            pltpu.VMEM((3, 3, width), jnp.float32),
            pltpu.VMEM((modes, width), jnp.float32),
            pltpu.VMEM((modes, width), jnp.float32),
            pltpu.VMEM((1, width), jnp.float32),
            pltpu.VMEM(((4 * modes + 10) * groups, LANES), jnp.float32),
            pltpu.VMEM(w_out.shape, jnp.bfloat16),
            pltpu.VMEM((3, (length + halo) * groups, LANES), jnp.float32),
            pltpu.VMEM((length * groups, LANES), jnp.float32),
            pltpu.VMEM((length * groups, LANES), jnp.float32),
            pltpu.VMEM((n_ctx, modes * groups, LANES), jnp.float32),
            pltpu.VMEM((n_ch, length, width), jnp.bfloat16),
            pltpu.VMEM((length, features), jnp.float32),
            pltpu.SemaphoreType.DMA((6,)),
            pltpu.SemaphoreType.DMA((1,)),
            pltpu.SemaphoreType.DMA((1,)),
            pltpu.SemaphoreType.DMA((n_ctx,)),
            pltpu.SemaphoreType.DMA((n_ctx,)),
            pltpu.SemaphoreType.DMA((2, n_ch, parts)),
            pltpu.SemaphoreType.DMA((n_ch, parts)),
        ],
        compiler_params=pltpu.CompilerParams(
            collective_id=0, has_side_effects=True, vmem_limit_bytes=63 * 1024 * 1024
        ),
        cost_estimate=pl.CostEstimate(
            flops=2 * length * total_width * features,
            bytes_accessed=2 * (total_width * features + 3 * width * length + length * features),
            transcendentals=0,
        ),
    )(proj, short_filter.transpose(0, 2, 1), residues.T, decays.T, skip[None, :], w_out)


def solution(mesh):
    in_specs = (
        P(None, "ch", "ctx"),
        P(None, "ch", None),
        P("ch", None),
        P("ch", None),
        P("ch"),
        P(None, "ch"),
    )
    dims_mesh = (mesh.shape["ctx"], mesh.shape["ch"])
    return jax.shard_map(
        functools.partial(per_device, dims_mesh),
        mesh=mesh, in_specs=in_specs, out_specs=P("ctx", "ch"), check_vma=False,
    )
```

```python
import functools

import jax
import jax.numpy as jnp
from jax import lax
from jax.experimental import pallas as pl
from jax.experimental.pallas import tpu as pltpu
from jax.sharding import PartitionSpec as P

MESH = pl.DeviceIdType.MESH
LANES = 128


def rounded(value):
    return value.astype(jnp.bfloat16).astype(jnp.float32)


def fused_kernel(
    dims, proj_hbm, short_hbm, weight_hbm, rate_hbm, skip_hbm, w_hbm, out_ref,
    proj_v, short_v, weight_v, rate_v, skip_v, coef_ref, w_v, mixed, signal, gate_rows, states, gathered, total,
    in_sem, halo_send, halo_recv, state_send, state_recv, send_sem, recv_sem,
):
    n_ctx, n_ch, length, groups, modes, halo, parts, features = dims
    width = groups * LANES
    rows = length // parts
    ctx = lax.axis_index("ctx")
    ch = lax.axis_index("ch")

    small = [
        pltpu.make_async_copy(source, target, in_sem.at[2 + k])
        for k, (source, target) in enumerate(
            [(rate_hbm, rate_v), (weight_hbm, weight_v), (short_hbm, short_v), (skip_hbm, skip_v)]
        )
    ]
    for copy in small:
        copy.start()
    load_proj = pltpu.make_async_copy(proj_hbm, proj_v, in_sem.at[0])
    load_proj.start()
    load_w = pltpu.make_async_copy(w_hbm, w_v, in_sem.at[1])
    load_w.start()

    barrier = pltpu.get_barrier_semaphore()

    def greet(step, carry):
        pl.semaphore_signal(
            barrier, inc=1, device_id={"ctx": lax.rem(ctx + step, n_ctx)}, device_id_type=MESH
        )
        return carry

    lax.fori_loop(1, n_ctx, greet, 0)

    @pl.when(ch > 0)
    def _():
        pl.semaphore_signal(barrier, inc=1, device_id={"ch": ch - 1}, device_id_type=MESH)

    @pl.when(ch < n_ch - 1)
    def _():
        pl.semaphore_signal(barrier, inc=1, device_id={"ch": ch + 1}, device_id_type=MESH)

    inner = jnp.where(ch > 0, 1, 0) + jnp.where(ch < n_ch - 1, 1, 0)

    for copy in small:
        copy.wait()

    def spread(base, value):
        for group in range(groups):
            coef_ref[pl.ds(base * groups + group, value.shape[0], stride=groups), :] = (
                value[:, group * LANES:(group + 1) * LANES]
            )

    rate = rate_v[...]
    spread(0, jnp.exp(-rate))
    spread(modes, weight_v[...] * jnp.sqrt(jnp.tanh(rate) * (1.0 + jnp.exp(-2.0 * rate))))
    spread(2 * modes, jnp.exp(-float(length) * rate))
    spread(3 * modes, jnp.exp(-float(length - 2) * rate))
    for i in range(3):
        spread(4 * modes + 3 * i, short_v[i])
    spread(4 * modes + 9, skip_v[...])

    def coef(index):
        return coef_ref[index * groups:(index + 1) * groups, :]

    decay = [coef(m) for m in range(modes)]
    taps = [[coef(4 * modes + 3 * i + m) for m in range(3)] for i in range(3)]
    skip = coef(4 * modes + 9)

    load_proj.wait()
    row_ids = lax.broadcasted_iota(jnp.int32, (length, length), 0)
    col_ids = lax.broadcasted_iota(jnp.int32, (length, length), 1)
    eye = jnp.where(row_ids == col_ids, 1.0, 0.0).astype(jnp.bfloat16)
    wide = min(width, 256)
    for i in range(3):
        for part in range(width // wide):
            turned = lax.dot_general(
                eye, proj_v[i, part * wide:(part + 1) * wide, :],
                (((1,), (1,)), ((), ())), preferred_element_type=jnp.float32,
            )
            for j in range(wide // LANES):
                group = part * (wide // LANES) + j
                mixed[i, pl.ds(halo * groups + group, length, stride=groups), :] = (
                    turned[:, j * LANES:(j + 1) * LANES]
                )

    pl.semaphore_wait(barrier, n_ctx - 1 + inner)

    edge = halo * groups
    halo_copy = pltpu.make_async_remote_copy(
        src_ref=mixed.at[:, pl.ds(length * groups, edge), :],
        dst_ref=mixed.at[:, pl.ds(0, edge), :],
        send_sem=halo_send.at[0],
        recv_sem=halo_recv.at[0],
        device_id={"ctx": lax.rem(ctx + 1, n_ctx)},
        device_id_type=MESH,
    )

    @pl.when(ctx < n_ctx - 1)
    def _():
        halo_copy.start()

    @pl.when(ctx == 0)
    def _():
        mixed[:, pl.ds(0, edge), :] = jnp.zeros((3, edge, LANES), jnp.float32)

    def short(i, t):
        def at(back):
            start = (t + halo - back) * groups
            if not isinstance(start, int):
                start = pl.multiple_of(start, groups)
            return mixed[i, pl.ds(start, groups), :]

        return taps[i][0] * at(0) + taps[i][1] * at(1) + taps[i][2] * at(2)

    def row_of(t):
        start = t * groups
        if not isinstance(start, int):
            start = pl.multiple_of(start, groups)
        return pl.ds(start, groups)

    def absorb(t, state):
        value = rounded(short(1, t) * short(2, t))
        signal[row_of(t), :] = value
        return tuple(d * s + value for d, s in zip(decay, state))

    empty = tuple(jnp.zeros((groups, LANES), jnp.float32) for _ in range(modes))
    state = empty
    for t in range(2, 8):
        state = absorb(t, state)
    state = lax.fori_loop(8, length, absorb, state, unroll=8)

    @pl.when(ctx > 0)
    def _():
        halo_copy.wait_recv()

    first = rounded(short(1, 0) * short(2, 0))
    second = rounded(short(1, 1) * short(2, 1))
    signal[row_of(0), :] = first
    signal[row_of(1), :] = second
    for m in range(modes):
        own = state[m] + coef(3 * modes + m) * (decay[m] * first + second)
        states[ctx, m * groups:(m + 1) * groups, :] = own

    def state_copy(source, target):
        return pltpu.make_async_remote_copy(
            src_ref=states.at[source],
            dst_ref=states.at[source],
            send_sem=state_send.at[target],
            recv_sem=state_recv.at[source],
            device_id={"ctx": target},
            device_id_type=MESH,
        )

    def send_state(target, carry):
        state_copy(ctx, target).start()
        return carry

    lax.fori_loop(ctx + 1, n_ctx, send_state, 0)

    def take_state(source, carried):
        state_copy(source, ctx).wait_recv()
        return tuple(
            coef(2 * modes + m) * carried[m] + states[source, m * groups:(m + 1) * groups, :]
            for m in range(modes)
        )

    state = lax.fori_loop(0, ctx, take_state, empty)

    gain = [coef(modes + m) for m in range(modes)]

    def advance(t, state):
        value = signal[row_of(t), :]
        state = tuple(d * s + value for d, s in zip(decay, state))
        terms = [g * s for g, s in zip(gain, state)]
        while len(terms) > 1:
            terms = [sum(terms[k:k + 2][1:], terms[k]) for k in range(0, len(terms), 2)]
        gate_rows[row_of(t), :] = rounded(short(0, t)) * (rounded(terms[0]) + skip * value)
        return state

    def block_copy(block, part, side):
        window = gathered.at[block, pl.ds(pl.multiple_of(part * rows, rows), rows), :]
        return pltpu.make_async_remote_copy(
            src_ref=window,
            dst_ref=window,
            send_sem=send_sem.at[side, block, part],
            recv_sem=recv_sem.at[block, part],
            device_id={"ch": jnp.clip(ch - 1 + 2 * side, 0, n_ch - 1)},
            device_id_type=MESH,
        )

    for part in range(parts):
        state = lax.fori_loop(part * rows, (part + 1) * rows, advance, state, unroll=4)
        for group in range(groups):
            tile = gate_rows[pl.ds(part * rows * groups + group, rows, stride=groups), :]
            gathered[ch, part * rows:(part + 1) * rows, group * LANES:(group + 1) * LANES] = (
                tile.astype(jnp.bfloat16)
            )

        @pl.when(ch > 0)
        def _():
            block_copy(ch, part, 0).start()

        @pl.when(ch < n_ch - 1)
        def _():
            block_copy(ch, part, 1).start()

    load_w.wait()

    slabs = min(parts, max(1, features // 256))
    slab = features // slabs

    def window(part):
        return pl.ds(pl.multiple_of(part * rows, rows), rows)

    def weight_rows(block):
        return pl.ds(pl.multiple_of(block * width, width), width)

    def add_columns(block, part, fresh):
        cols = pl.ds(pl.multiple_of(part * slab, slab), slab)
        value = jnp.dot(
            gathered[block], w_v[weight_rows(block), cols], preferred_element_type=jnp.float32
        )
        if fresh:
            total[:, cols] = value
        else:
            total[:, cols] += value

    def add_rows(block, part):
        total[window(part), :] += jnp.dot(
            gathered[block, window(part), :], w_v[weight_rows(block), :],
            preferred_element_type=jnp.float32,
        )

    def block_at(distance, side):
        if side == 0:
            return ch + distance, ch + distance < n_ch
        return ch - distance, ch >= distance

    for distance in range(1, n_ch):
        last = distance == n_ch - 1

        def arrive(part):
            for side in (0, 1):
                block, here = block_at(distance, side)
                further = (ch > 0) if side == 0 else (ch < n_ch - 1)

                @pl.when(here)
                def _():
                    block_copy(block, part, side).wait_recv()

                @pl.when(here & further)
                def _():
                    block_copy(block, part, side).start()

        def multiply_before(part):
            if distance == 1:
                @pl.when(part < slabs)
                def _():
                    add_columns(ch, part, True)
                return
            for side in (0, 1):
                block, here = block_at(distance - 1, side)

                @pl.when(here & (part < slabs))
                def _():
                    add_columns(block, part, False)

        def multiply_rows(part):
            for side in (0, 1):
                block, here = block_at(distance, side)

                @pl.when(here)
                def _():
                    add_rows(block, part)

        def one_part(part, carry):
            if last and distance > 1:
                multiply_before(part)
                arrive(part)
                multiply_rows(part)
            else:
                arrive(part)
                multiply_before(part)
            return carry

        def last_rows(part, carry):
            multiply_rows(part)
            return carry

        lax.fori_loop(0, parts, one_part, 0)
        if last and distance == 1:
            lax.fori_loop(0, parts, last_rows, 0)

    out_ref[...] = total[...].astype(jnp.bfloat16)

    @pl.when(ctx < n_ctx - 1)
    def _():
        halo_copy.wait_send()

    def sent_state(target, carry):
        state_copy(ctx, target).wait_send()
        return carry

    lax.fori_loop(ctx + 1, n_ctx, sent_state, 0)

    def sent_left(block, carry):
        for part in range(parts):
            block_copy(block, part, 0).wait_send()
        return carry

    def sent_right(block, carry):
        for part in range(parts):
            block_copy(block, part, 1).wait_send()
        return carry

    @pl.when(ch > 0)
    def _():
        lax.fori_loop(ch, n_ch, sent_left, 0)

    @pl.when(ch < n_ch - 1)
    def _():
        lax.fori_loop(0, ch + 1, sent_right, 0)


def per_device(dims_mesh, proj, short_filter, residues, decays, skip, w_out):
    n_ctx, n_ch = dims_mesh
    _, width, length = proj.shape
    modes = residues.shape[1]
    groups = width // LANES
    halo = max(2, 8 // groups)
    parts = 4
    features = w_out.shape[1]
    dims = (n_ctx, n_ch, length, groups, modes, halo, parts, features)
    total_width = w_out.shape[0]
    return pl.pallas_call(
        functools.partial(fused_kernel, dims),
        out_shape=jax.ShapeDtypeStruct((length, features), jnp.bfloat16),
        in_specs=[
            pl.BlockSpec(memory_space=pl.ANY),
        ] * 6,
        out_specs=pl.BlockSpec(memory_space=pltpu.VMEM),
        scratch_shapes=[
            pltpu.VMEM(proj.shape, jnp.bfloat16),
            pltpu.VMEM((3, 3, width), jnp.float32),
            pltpu.VMEM((modes, width), jnp.float32),
            pltpu.VMEM((modes, width), jnp.float32),
            pltpu.VMEM((1, width), jnp.float32),
            pltpu.VMEM(((4 * modes + 10) * groups, LANES), jnp.float32),
            pltpu.VMEM(w_out.shape, jnp.bfloat16),
            pltpu.VMEM((3, (length + halo) * groups, LANES), jnp.float32),
            pltpu.VMEM((length * groups, LANES), jnp.float32),
            pltpu.VMEM((length * groups, LANES), jnp.float32),
            pltpu.VMEM((n_ctx, modes * groups, LANES), jnp.float32),
            pltpu.VMEM((n_ch, length, width), jnp.bfloat16),
            pltpu.VMEM((length, features), jnp.float32),
            pltpu.SemaphoreType.DMA((6,)),
            pltpu.SemaphoreType.DMA((1,)),
            pltpu.SemaphoreType.DMA((1,)),
            pltpu.SemaphoreType.DMA((n_ctx,)),
            pltpu.SemaphoreType.DMA((n_ctx,)),
            pltpu.SemaphoreType.DMA((2, n_ch, parts)),
            pltpu.SemaphoreType.DMA((n_ch, parts)),
        ],
        compiler_params=pltpu.CompilerParams(
            collective_id=0, has_side_effects=True, vmem_limit_bytes=62 * 1024 * 1024 + 640 * 1024
        ),
        cost_estimate=pl.CostEstimate(
            flops=2 * length * total_width * features,
            bytes_accessed=2 * (total_width * features + 3 * width * length + length * features),
            transcendentals=0,
        ),
    )(proj, short_filter.transpose(0, 2, 1), residues.T, decays.T, skip[None, :], w_out)


def solution(mesh):
    in_specs = (
        P(None, "ch", "ctx"),
        P(None, "ch", None),
        P("ch", None),
        P("ch", None),
        P("ch"),
        P(None, "ch"),
    )
    dims_mesh = (mesh.shape["ctx"], mesh.shape["ch"])
    return jax.shard_map(
        functools.partial(per_device, dims_mesh),
        mesh=mesh, in_specs=in_specs, out_specs=P("ctx", "ch"), check_vma=False,
    )
```

```python
import functools

import jax
import jax.numpy as jnp
from jax import lax
from jax.experimental import pallas as pl
from jax.experimental.pallas import tpu as pltpu
from jax.sharding import PartitionSpec as P

MESH = pl.DeviceIdType.MESH
LANES = 128


def rounded(value):
    return value.astype(jnp.bfloat16).astype(jnp.float32)


def fused_kernel(
    dims, proj_hbm, short_hbm, weight_hbm, rate_hbm, skip_hbm, w_hbm, out_ref,
    proj_v, short_v, weight_v, rate_v, skip_v, coef_ref, w_v, mixed, signal, query, gate_rows, pair, chips,
    gathered, total,
    in_sem, halo_send, halo_recv, pair_send, pair_recv, state_send, state_recv, send_sem, recv_sem,
):
    n_ctx, n_ch, length, groups, modes, halo, parts, features = dims
    width = groups * LANES
    rows = length // parts
    ctx = lax.axis_index("ctx")
    ch = lax.axis_index("ch")

    small = [
        pltpu.make_async_copy(source, target, in_sem.at[2 + k])
        for k, (source, target) in enumerate(
            [(rate_hbm, rate_v), (weight_hbm, weight_v), (short_hbm, short_v), (skip_hbm, skip_v)]
        )
    ]
    for copy in small:
        copy.start()
    load_proj = pltpu.make_async_copy(proj_hbm, proj_v, in_sem.at[0])
    load_proj.start()
    load_w = pltpu.make_async_copy(w_hbm, w_v, in_sem.at[1])
    load_w.start()

    barrier = pltpu.get_barrier_semaphore()

    def greet(step, carry):
        pl.semaphore_signal(
            barrier, inc=1, device_id={"ctx": lax.rem(ctx + step, n_ctx)}, device_id_type=MESH
        )
        return carry

    lax.fori_loop(1, n_ctx, greet, 0)

    @pl.when(ch > 0)
    def _():
        pl.semaphore_signal(barrier, inc=1, device_id={"ch": ch - 1}, device_id_type=MESH)

    @pl.when(ch < n_ch - 1)
    def _():
        pl.semaphore_signal(barrier, inc=1, device_id={"ch": ch + 1}, device_id_type=MESH)

    inner = jnp.where(ch > 0, 1, 0) + jnp.where(ch < n_ch - 1, 1, 0)

    for copy in small:
        copy.wait()

    def spread(base, value):
        for group in range(groups):
            coef_ref[pl.ds(base * groups + group, value.shape[0], stride=groups), :] = (
                value[:, group * LANES:(group + 1) * LANES]
            )

    rate = rate_v[...]
    spread(0, jnp.exp(-rate))
    spread(modes, weight_v[...] * jnp.sqrt(jnp.tanh(rate) * (1.0 + jnp.exp(-2.0 * rate))))
    spread(2 * modes, jnp.exp(-float(length) * rate))
    spread(3 * modes, jnp.exp(-float(length - 2) * rate))
    for i in range(3):
        spread(4 * modes + 3 * i, short_v[i])
    spread(4 * modes + 9, skip_v[...])

    def coef(index):
        return coef_ref[index * groups:(index + 1) * groups, :]

    decay = [coef(m) for m in range(modes)]
    taps = [[coef(4 * modes + 3 * i + m) for m in range(3)] for i in range(3)]
    skip = coef(4 * modes + 9)

    load_proj.wait()
    row_ids = lax.broadcasted_iota(jnp.int32, (length, length), 0)
    col_ids = lax.broadcasted_iota(jnp.int32, (length, length), 1)
    eye = jnp.where(row_ids == col_ids, 1.0, 0.0).astype(jnp.bfloat16)
    wide = min(width, 256)

    def turn(i):
        for part in range(width // wide):
            turned = lax.dot_general(
                eye, proj_v[i, part * wide:(part + 1) * wide, :],
                (((1,), (1,)), ((), ())), preferred_element_type=jnp.float32,
            )
            for j in range(wide // LANES):
                group = part * (wide // LANES) + j
                mixed[i, pl.ds(halo * groups + group, length, stride=groups), :] = (
                    turned[:, j * LANES:(j + 1) * LANES]
                )

    turn(1)
    turn(2)

    pl.semaphore_wait(barrier, n_ctx - 1 + inner)

    edge = halo * groups

    def halo_copy(first, count):
        return pltpu.make_async_remote_copy(
            src_ref=mixed.at[first:first + count, pl.ds(length * groups, edge), :],
            dst_ref=mixed.at[first:first + count, pl.ds(0, edge), :],
            send_sem=halo_send.at[first],
            recv_sem=halo_recv.at[first],
            device_id={"ctx": lax.rem(ctx + 1, n_ctx)},
            device_id_type=MESH,
        )

    @pl.when(ctx < n_ctx - 1)
    def _():
        halo_copy(1, 2).start()

    @pl.when(ctx == 0)
    def _():
        mixed[:, pl.ds(0, edge), :] = jnp.zeros((3, edge, LANES), jnp.float32)

    def short(i, t):
        def at(back):
            start = (t + halo - back) * groups
            if not isinstance(start, int):
                start = pl.multiple_of(start, groups)
            return mixed[i, pl.ds(start, groups), :]

        return taps[i][0] * at(0) + taps[i][1] * at(1) + taps[i][2] * at(2)

    def row_of(t):
        start = t * groups
        if not isinstance(start, int):
            start = pl.multiple_of(start, groups)
        return pl.ds(start, groups)

    def absorb(t, state):
        value = rounded(short(1, t) * short(2, t))
        signal[row_of(t), :] = value
        return tuple(d * s + value for d, s in zip(decay, state))

    empty = tuple(jnp.zeros((groups, LANES), jnp.float32) for _ in range(modes))
    state = empty
    for t in range(2, 8):
        state = absorb(t, state)
    state = lax.fori_loop(8, length, absorb, state, unroll=8)

    @pl.when(ctx > 0)
    def _():
        halo_copy(1, 2).wait_recv()

    first = rounded(short(1, 0) * short(2, 0))
    second = rounded(short(1, 1) * short(2, 1))
    signal[row_of(0), :] = first
    signal[row_of(1), :] = second

    chip, core = ctx // 2, lax.rem(ctx, 2)
    half = modes * groups // 2
    for m in range(modes):
        own = state[m] + coef(3 * modes + m) * (decay[m] * first + second)
        pair[core, m * groups:(m + 1) * groups, :] = own

    def pair_copy(source):
        return pltpu.make_async_remote_copy(
            src_ref=pair.at[source],
            dst_ref=pair.at[source],
            send_sem=pair_send.at[0],
            recv_sem=pair_recv.at[0],
            device_id={"ctx": 2 * chip + 1 - core},
            device_id_type=MESH,
        )

    pair_copy(core).start()
    turn(0)

    @pl.when(ctx < n_ctx - 1)
    def _():
        halo_copy(0, 1).start()

    pair_copy(1 - core).wait_recv()

    def half_rows(which, base=0):
        return pl.ds(pl.multiple_of(base + which * half, half), half)

    chips[chip, half_rows(core), :] = (
        coef_ref[half_rows(core, 2 * modes * groups), :] * pair[0, half_rows(core), :]
        + pair[1, half_rows(core), :]
    )

    def chip_copy(source, which, target):
        window = chips.at[source, half_rows(which), :]
        return pltpu.make_async_remote_copy(
            src_ref=window,
            dst_ref=window,
            send_sem=state_send.at[target],
            recv_sem=state_recv.at[source, which],
            device_id={"ctx": target},
            device_id_type=MESH,
        )

    def send_chip(target, carry):
        chip_copy(chip, core, target).start()
        return carry

    lax.fori_loop(2 * chip + 2, n_ctx, send_chip, 0)

    gain = [coef(modes + m) for m in range(modes)]

    def summed(terms):
        while len(terms) > 1:
            terms = [sum(terms[k:k + 2][1:], terms[k]) for k in range(0, len(terms), 2)]
        return terms[0]

    def advance(t, state):
        value = signal[row_of(t), :]
        state = tuple(d * s + value for d, s in zip(decay, state))
        gate_rows[row_of(t), :] = summed([g * s for g, s in zip(gain, state)])
        return state

    def advance_query(t, state):
        query[row_of(t), :] = rounded(short(0, t))
        return advance(t, state)

    state = empty
    for t in range(2):
        state = advance(t, state)
    for t in range(2, 4):
        state = advance_query(t, state)
    lax.fori_loop(4, length, advance_query, state, unroll=4)

    @pl.when(ctx > 0)
    def _():
        halo_copy(0, 1).wait_recv()

    for t in range(2):
        query[row_of(t), :] = rounded(short(0, t))

    def take_chip(source, carried):
        for which in range(2):
            chip_copy(source, which, ctx).wait_recv()
        return tuple(
            coef(2 * modes + m) * (coef(2 * modes + m) * carried[m])
            + chips[source, m * groups:(m + 1) * groups, :]
            for m in range(modes)
        )

    state = lax.fori_loop(0, chip, take_chip, empty)
    odd = core == 1
    state = tuple(
        gain[m] * jnp.where(
            odd,
            coef(2 * modes + m) * state[m] + pair[0, m * groups:(m + 1) * groups, :],
            state[m],
        )
        for m in range(modes)
    )

    def finish(t, state):
        state = tuple(d * s for d, s in zip(decay, state))
        conv = rounded(gate_rows[row_of(t), :] + summed(list(state)))
        gate_rows[row_of(t), :] = query[row_of(t), :] * (conv + skip * signal[row_of(t), :])
        return state

    def block_copy(block, part, side):
        window = gathered.at[block, pl.ds(pl.multiple_of(part * rows, rows), rows), :]
        return pltpu.make_async_remote_copy(
            src_ref=window,
            dst_ref=window,
            send_sem=send_sem.at[side, block, part],
            recv_sem=recv_sem.at[block, part],
            device_id={"ch": jnp.clip(ch - 1 + 2 * side, 0, n_ch - 1)},
            device_id_type=MESH,
        )

    for part in range(parts):
        state = lax.fori_loop(part * rows, (part + 1) * rows, finish, state, unroll=8)
        for group in range(groups):
            tile = gate_rows[pl.ds(part * rows * groups + group, rows, stride=groups), :]
            gathered[ch, part * rows:(part + 1) * rows, group * LANES:(group + 1) * LANES] = (
                tile.astype(jnp.bfloat16)
            )

        @pl.when(ch > 0)
        def _():
            block_copy(ch, part, 0).start()

        @pl.when(ch < n_ch - 1)
        def _():
            block_copy(ch, part, 1).start()

    load_w.wait()

    slabs = min(parts, max(1, features // 256))
    slab = features // slabs

    def window(part):
        return pl.ds(pl.multiple_of(part * rows, rows), rows)

    def weight_rows(block):
        return pl.ds(pl.multiple_of(block * width, width), width)

    def add_columns(block, part, fresh):
        cols = pl.ds(pl.multiple_of(part * slab, slab), slab)
        value = jnp.dot(
            gathered[block], w_v[weight_rows(block), cols], preferred_element_type=jnp.float32
        )
        if fresh:
            total[:, cols] = value
        else:
            total[:, cols] += value

    def add_rows(block, part):
        total[window(part), :] += jnp.dot(
            gathered[block, window(part), :], w_v[weight_rows(block), :],
            preferred_element_type=jnp.float32,
        )

    def block_at(distance, side):
        if side == 0:
            return ch + distance, ch + distance < n_ch
        return ch - distance, ch >= distance

    for distance in range(1, n_ch):
        last = distance == n_ch - 1

        def arrive(part):
            for side in (0, 1):
                block, here = block_at(distance, side)
                further = (ch > 0) if side == 0 else (ch < n_ch - 1)

                @pl.when(here)
                def _():
                    block_copy(block, part, side).wait_recv()

                @pl.when(here & further)
                def _():
                    block_copy(block, part, side).start()

        def multiply_before(part):
            if distance == 1:
                @pl.when(part < slabs)
                def _():
                    add_columns(ch, part, True)
                return
            for side in (0, 1):
                block, here = block_at(distance - 1, side)

                @pl.when(here & (part < slabs))
                def _():
                    add_columns(block, part, False)

        def multiply_rows(part):
            for side in (0, 1):
                block, here = block_at(distance, side)

                @pl.when(here)
                def _():
                    add_rows(block, part)

        def one_part(part, carry):
            if last and distance > 1:
                multiply_before(part)
                arrive(part)
                multiply_rows(part)
            else:
                arrive(part)
                multiply_before(part)
            return carry

        def last_rows(part, carry):
            multiply_rows(part)
            return carry

        lax.fori_loop(0, parts, one_part, 0)
        if last and distance == 1:
            lax.fori_loop(0, parts, last_rows, 0)

    out_ref[...] = total[...].astype(jnp.bfloat16)

    @pl.when(ctx < n_ctx - 1)
    def _():
        halo_copy(1, 2).wait_send()
        halo_copy(0, 1).wait_send()

    pair_copy(core).wait_send()

    def sent_chip(target, carry):
        chip_copy(chip, core, target).wait_send()
        return carry

    lax.fori_loop(2 * chip + 2, n_ctx, sent_chip, 0)

    def sent_left(block, carry):
        for part in range(parts):
            block_copy(block, part, 0).wait_send()
        return carry

    def sent_right(block, carry):
        for part in range(parts):
            block_copy(block, part, 1).wait_send()
        return carry

    @pl.when(ch > 0)
    def _():
        lax.fori_loop(ch, n_ch, sent_left, 0)

    @pl.when(ch < n_ch - 1)
    def _():
        lax.fori_loop(0, ch + 1, sent_right, 0)


def per_device(dims_mesh, proj, short_filter, residues, decays, skip, w_out):
    n_ctx, n_ch = dims_mesh
    _, width, length = proj.shape
    modes = residues.shape[1]
    groups = width // LANES
    halo = max(2, 8 // groups)
    parts = 8
    features = w_out.shape[1]
    dims = (n_ctx, n_ch, length, groups, modes, halo, parts, features)
    total_width = w_out.shape[0]
    return pl.pallas_call(
        functools.partial(fused_kernel, dims),
        out_shape=jax.ShapeDtypeStruct((length, features), jnp.bfloat16),
        in_specs=[
            pl.BlockSpec(memory_space=pl.ANY),
        ] * 6,
        out_specs=pl.BlockSpec(memory_space=pltpu.VMEM),
        scratch_shapes=[
            pltpu.VMEM(proj.shape, jnp.bfloat16),
            pltpu.VMEM((3, 3, width), jnp.float32),
            pltpu.VMEM((modes, width), jnp.float32),
            pltpu.VMEM((modes, width), jnp.float32),
            pltpu.VMEM((1, width), jnp.float32),
            pltpu.VMEM(((4 * modes + 10) * groups, LANES), jnp.float32),
            pltpu.VMEM(w_out.shape, jnp.bfloat16),
            pltpu.VMEM((3, (length + halo) * groups, LANES), jnp.float32),
            pltpu.VMEM((length * groups, LANES), jnp.float32),
            pltpu.VMEM((length * groups, LANES), jnp.float32),
            pltpu.VMEM((length * groups, LANES), jnp.float32),
            pltpu.VMEM((2, modes * groups, LANES), jnp.float32),
            pltpu.VMEM((n_ctx // 2, modes * groups, LANES), jnp.float32),
            pltpu.VMEM((n_ch, length, width), jnp.bfloat16),
            pltpu.VMEM((length, features), jnp.float32),
            pltpu.SemaphoreType.DMA((6,)),
            pltpu.SemaphoreType.DMA((2,)),
            pltpu.SemaphoreType.DMA((2,)),
            pltpu.SemaphoreType.DMA((1,)),
            pltpu.SemaphoreType.DMA((1,)),
            pltpu.SemaphoreType.DMA((n_ctx,)),
            pltpu.SemaphoreType.DMA((n_ctx // 2, 2)),
            pltpu.SemaphoreType.DMA((2, n_ch, parts)),
            pltpu.SemaphoreType.DMA((n_ch, parts)),
        ],
        compiler_params=pltpu.CompilerParams(
            collective_id=0, has_side_effects=True, vmem_limit_bytes=52 * 1024 * 1024
        ),
        cost_estimate=pl.CostEstimate(
            flops=2 * length * total_width * features,
            bytes_accessed=2 * (total_width * features + 3 * width * length + length * features),
            transcendentals=0,
        ),
    )(proj, short_filter.transpose(0, 2, 1), residues.T, decays.T, skip[None, :], w_out)


def solution(mesh):
    in_specs = (
        P(None, "ch", "ctx"),
        P(None, "ch", None),
        P("ch", None),
        P("ch", None),
        P("ch"),
        P(None, "ch"),
    )
    dims_mesh = (mesh.shape["ctx"], mesh.shape["ch"])
    return jax.shard_map(
        functools.partial(per_device, dims_mesh),
        mesh=mesh, in_specs=in_specs, out_specs=P("ctx", "ch"), check_vma=False,
    )
```

```python
import functools

import jax
import jax.numpy as jnp
from jax import lax
from jax.experimental import pallas as pl
from jax.experimental.pallas import tpu as pltpu
from jax.sharding import PartitionSpec as P

MESH = pl.DeviceIdType.MESH
LANES = 128


def rounded(value):
    return value.astype(jnp.bfloat16).astype(jnp.float32)


def fused_kernel(
    dims, proj_hbm, short_hbm, weight_hbm, rate_hbm, skip_hbm, w_hbm, out_ref,
    proj_v, short_v, weight_v, rate_v, skip_v, coef_ref, w_v, mixed, signal, query, gate_rows, pair, chips,
    gathered, total,
    in_sem, halo_send, halo_recv, pair_send, pair_recv, state_send, state_recv, send_sem, recv_sem,
):
    n_ctx, n_ch, length, groups, modes, halo, parts, features = dims
    width = groups * LANES
    rows = length // parts
    ctx = lax.axis_index("ctx")
    ch = lax.axis_index("ch")

    small = [
        pltpu.make_async_copy(source, target, in_sem.at[2 + k])
        for k, (source, target) in enumerate(
            [(rate_hbm, rate_v), (weight_hbm, weight_v), (short_hbm, short_v), (skip_hbm, skip_v)]
        )
    ]
    for copy in small:
        copy.start()
    load_proj = pltpu.make_async_copy(proj_hbm, proj_v, in_sem.at[0])
    load_proj.start()
    load_w = pltpu.make_async_copy(w_hbm, w_v, in_sem.at[1])
    load_w.start()

    barrier = pltpu.get_barrier_semaphore()

    def greet(step, carry):
        pl.semaphore_signal(
            barrier, inc=1, device_id={"ctx": lax.rem(ctx + step, n_ctx)}, device_id_type=MESH
        )
        return carry

    lax.fori_loop(1, n_ctx, greet, 0)

    @pl.when(ch > 0)
    def _():
        pl.semaphore_signal(barrier, inc=1, device_id={"ch": ch - 1}, device_id_type=MESH)

    @pl.when(ch < n_ch - 1)
    def _():
        pl.semaphore_signal(barrier, inc=1, device_id={"ch": ch + 1}, device_id_type=MESH)

    inner = jnp.where(ch > 0, 1, 0) + jnp.where(ch < n_ch - 1, 1, 0)

    for copy in small:
        copy.wait()

    def spread(base, value):
        for group in range(groups):
            coef_ref[pl.ds(base * groups + group, value.shape[0], stride=groups), :] = (
                value[:, group * LANES:(group + 1) * LANES]
            )

    rate = rate_v[...]
    spread(0, jnp.exp(-rate))
    spread(modes, weight_v[...] * jnp.sqrt(jnp.tanh(rate) * (1.0 + jnp.exp(-2.0 * rate))))
    spread(2 * modes, jnp.exp(-float(length) * rate))
    spread(3 * modes, jnp.exp(-float(length - 2) * rate))
    for i in range(3):
        spread(4 * modes + 3 * i, short_v[i])
    spread(4 * modes + 9, skip_v[...])

    def coef(index):
        return coef_ref[index * groups:(index + 1) * groups, :]

    decay = [coef(m) for m in range(modes)]
    taps = [[coef(4 * modes + 3 * i + m) for m in range(3)] for i in range(3)]
    skip = coef(4 * modes + 9)

    load_proj.wait()
    row_ids = lax.broadcasted_iota(jnp.int32, (length, length), 0)
    col_ids = lax.broadcasted_iota(jnp.int32, (length, length), 1)
    eye = jnp.where(row_ids == col_ids, 1.0, 0.0).astype(jnp.bfloat16)
    wide = min(width, 256)

    def turn(i):
        for part in range(width // wide):
            turned = lax.dot_general(
                eye, proj_v[i, part * wide:(part + 1) * wide, :],
                (((1,), (1,)), ((), ())), preferred_element_type=jnp.float32,
            )
            for j in range(wide // LANES):
                group = part * (wide // LANES) + j
                mixed[i, pl.ds(halo * groups + group, length, stride=groups), :] = (
                    turned[:, j * LANES:(j + 1) * LANES]
                )

    turn(1)
    turn(2)

    pl.semaphore_wait(barrier, n_ctx - 1 + inner)

    edge = halo * groups

    def halo_copy(first, count):
        return pltpu.make_async_remote_copy(
            src_ref=mixed.at[first:first + count, pl.ds(length * groups, edge), :],
            dst_ref=mixed.at[first:first + count, pl.ds(0, edge), :],
            send_sem=halo_send.at[first],
            recv_sem=halo_recv.at[first],
            device_id={"ctx": lax.rem(ctx + 1, n_ctx)},
            device_id_type=MESH,
        )

    @pl.when(ctx < n_ctx - 1)
    def _():
        halo_copy(1, 2).start()

    @pl.when(ctx == 0)
    def _():
        mixed[:, pl.ds(0, edge), :] = jnp.zeros((3, edge, LANES), jnp.float32)

    def short(i, t):
        def at(back):
            start = (t + halo - back) * groups
            if not isinstance(start, int):
                start = pl.multiple_of(start, groups)
            return mixed[i, pl.ds(start, groups), :]

        return taps[i][0] * at(0) + taps[i][1] * at(1) + taps[i][2] * at(2)

    def row_of(t):
        start = t * groups
        if not isinstance(start, int):
            start = pl.multiple_of(start, groups)
        return pl.ds(start, groups)

    def absorb(t, state):
        value = rounded(short(1, t) * short(2, t))
        signal[row_of(t), :] = value
        return tuple(d * s + value for d, s in zip(decay, state))

    empty = tuple(jnp.zeros((groups, LANES), jnp.float32) for _ in range(modes))
    state = empty
    for t in range(2, 8):
        state = absorb(t, state)
    state = lax.fori_loop(8, length, absorb, state, unroll=8)

    @pl.when(ctx > 0)
    def _():
        halo_copy(1, 2).wait_recv()

    first = rounded(short(1, 0) * short(2, 0))
    second = rounded(short(1, 1) * short(2, 1))
    signal[row_of(0), :] = first
    signal[row_of(1), :] = second

    chip, core = ctx // 2, lax.rem(ctx, 2)
    half = modes * groups // 2
    for m in range(modes):
        own = state[m] + coef(3 * modes + m) * (decay[m] * first + second)
        pair[core, m * groups:(m + 1) * groups, :] = own

    def pair_copy(source):
        return pltpu.make_async_remote_copy(
            src_ref=pair.at[source],
            dst_ref=pair.at[source],
            send_sem=pair_send.at[0],
            recv_sem=pair_recv.at[0],
            device_id={"ctx": 2 * chip + 1 - core},
            device_id_type=MESH,
        )

    pair_copy(core).start()
    turn(0)

    @pl.when(ctx < n_ctx - 1)
    def _():
        halo_copy(0, 1).start()

    pair_copy(1 - core).wait_recv()

    def half_rows(which, base=0):
        return pl.ds(pl.multiple_of(base + which * half, half), half)

    chips[chip, half_rows(core), :] = (
        coef_ref[half_rows(core, 2 * modes * groups), :] * pair[0, half_rows(core), :]
        + pair[1, half_rows(core), :]
    )

    def chip_copy(source, which, target):
        window = chips.at[source, half_rows(which), :]
        return pltpu.make_async_remote_copy(
            src_ref=window,
            dst_ref=window,
            send_sem=state_send.at[target],
            recv_sem=state_recv.at[source, which],
            device_id={"ctx": target},
            device_id_type=MESH,
        )

    def send_chip(target, carry):
        chip_copy(chip, core, target).start()
        return carry

    lax.fori_loop(2 * chip + 2, n_ctx, send_chip, 0)

    def project(t, carry):
        query[row_of(t), :] = rounded(short(0, t))
        return carry

    for t in range(2, 8):
        project(t, 0)
    lax.fori_loop(8, length, project, 0, unroll=8)

    @pl.when(ctx > 0)
    def _():
        halo_copy(0, 1).wait_recv()

    for t in range(2):
        query[row_of(t), :] = rounded(short(0, t))

    def take_chip(source, carried):
        for which in range(2):
            chip_copy(source, which, ctx).wait_recv()
        return tuple(
            coef(2 * modes + m) * (coef(2 * modes + m) * carried[m])
            + chips[source, m * groups:(m + 1) * groups, :]
            for m in range(modes)
        )

    state = lax.fori_loop(0, chip, take_chip, empty)
    odd = core == 1
    state = tuple(
        jnp.where(
            odd,
            coef(2 * modes + m) * state[m] + pair[0, m * groups:(m + 1) * groups, :],
            state[m],
        )
        for m in range(modes)
    )
    gain = [coef(modes + m) for m in range(modes)]

    def summed(terms):
        while len(terms) > 1:
            terms = [sum(terms[k:k + 2][1:], terms[k]) for k in range(0, len(terms), 2)]
        return terms[0]

    def finish(t, state):
        value = signal[row_of(t), :]
        state = tuple(d * s + value for d, s in zip(decay, state))
        conv = rounded(summed([g * s for g, s in zip(gain, state)]))
        gate_rows[row_of(t), :] = query[row_of(t), :] * (conv + skip * value)
        return state

    def block_copy(block, part, side):
        window = gathered.at[block, pl.ds(pl.multiple_of(part * rows, rows), rows), :]
        return pltpu.make_async_remote_copy(
            src_ref=window,
            dst_ref=window,
            send_sem=send_sem.at[side, block, part],
            recv_sem=recv_sem.at[block, part],
            device_id={"ch": jnp.clip(ch - 1 + 2 * side, 0, n_ch - 1)},
            device_id_type=MESH,
        )

    for part in range(parts):
        state = lax.fori_loop(part * rows, (part + 1) * rows, finish, state, unroll=4)
        for group in range(groups):
            tile = gate_rows[pl.ds(part * rows * groups + group, rows, stride=groups), :]
            gathered[ch, part * rows:(part + 1) * rows, group * LANES:(group + 1) * LANES] = (
                tile.astype(jnp.bfloat16)
            )

        @pl.when(ch > 0)
        def _():
            block_copy(ch, part, 0).start()

        @pl.when(ch < n_ch - 1)
        def _():
            block_copy(ch, part, 1).start()

    load_w.wait()

    slabs = min(parts, max(1, features // 256))
    slab = features // slabs

    def window(part):
        return pl.ds(pl.multiple_of(part * rows, rows), rows)

    def weight_rows(block):
        return pl.ds(pl.multiple_of(block * width, width), width)

    def add_columns(block, part, fresh):
        cols = pl.ds(pl.multiple_of(part * slab, slab), slab)
        value = jnp.dot(
            gathered[block], w_v[weight_rows(block), cols], preferred_element_type=jnp.float32
        )
        if fresh:
            total[:, cols] = value
        else:
            total[:, cols] += value

    def add_rows(block, part):
        total[window(part), :] += jnp.dot(
            gathered[block, window(part), :], w_v[weight_rows(block), :],
            preferred_element_type=jnp.float32,
        )

    def block_at(distance, side):
        if side == 0:
            return ch + distance, ch + distance < n_ch
        return ch - distance, ch >= distance

    for distance in range(1, n_ch):
        last = distance == n_ch - 1

        def arrive(part):
            for side in (0, 1):
                block, here = block_at(distance, side)
                further = (ch > 0) if side == 0 else (ch < n_ch - 1)

                @pl.when(here)
                def _():
                    block_copy(block, part, side).wait_recv()

                @pl.when(here & further)
                def _():
                    block_copy(block, part, side).start()

        def multiply_before(part):
            if distance == 1:
                @pl.when(part < slabs)
                def _():
                    add_columns(ch, part, True)
                return
            for side in (0, 1):
                block, here = block_at(distance - 1, side)

                @pl.when(here & (part < slabs))
                def _():
                    add_columns(block, part, False)

        def multiply_rows(part):
            for side in (0, 1):
                block, here = block_at(distance, side)

                @pl.when(here)
                def _():
                    add_rows(block, part)

        def one_part(part, carry):
            if last and distance > 1:
                multiply_before(part)
                arrive(part)
                multiply_rows(part)
            else:
                arrive(part)
                multiply_before(part)
            return carry

        def last_rows(part, carry):
            multiply_rows(part)
            return carry

        lax.fori_loop(0, parts, one_part, 0)
        if last and distance == 1:
            lax.fori_loop(0, parts, last_rows, 0)

    out_ref[...] = total[...].astype(jnp.bfloat16)

    @pl.when(ctx < n_ctx - 1)
    def _():
        halo_copy(1, 2).wait_send()
        halo_copy(0, 1).wait_send()

    pair_copy(core).wait_send()

    def sent_chip(target, carry):
        chip_copy(chip, core, target).wait_send()
        return carry

    lax.fori_loop(2 * chip + 2, n_ctx, sent_chip, 0)

    def sent_left(block, carry):
        for part in range(parts):
            block_copy(block, part, 0).wait_send()
        return carry

    def sent_right(block, carry):
        for part in range(parts):
            block_copy(block, part, 1).wait_send()
        return carry

    @pl.when(ch > 0)
    def _():
        lax.fori_loop(ch, n_ch, sent_left, 0)

    @pl.when(ch < n_ch - 1)
    def _():
        lax.fori_loop(0, ch + 1, sent_right, 0)


def per_device(dims_mesh, proj, short_filter, residues, decays, skip, w_out):
    n_ctx, n_ch = dims_mesh
    _, width, length = proj.shape
    modes = residues.shape[1]
    groups = width // LANES
    halo = max(2, 8 // groups)
    parts = 8
    features = w_out.shape[1]
    dims = (n_ctx, n_ch, length, groups, modes, halo, parts, features)
    total_width = w_out.shape[0]
    return pl.pallas_call(
        functools.partial(fused_kernel, dims),
        out_shape=jax.ShapeDtypeStruct((length, features), jnp.bfloat16),
        in_specs=[
            pl.BlockSpec(memory_space=pl.ANY),
        ] * 6,
        out_specs=pl.BlockSpec(memory_space=pltpu.VMEM),
        scratch_shapes=[
            pltpu.VMEM(proj.shape, jnp.bfloat16),
            pltpu.VMEM((3, 3, width), jnp.float32),
            pltpu.VMEM((modes, width), jnp.float32),
            pltpu.VMEM((modes, width), jnp.float32),
            pltpu.VMEM((1, width), jnp.float32),
            pltpu.VMEM(((4 * modes + 10) * groups, LANES), jnp.float32),
            pltpu.VMEM(w_out.shape, jnp.bfloat16),
            pltpu.VMEM((3, (length + halo) * groups, LANES), jnp.float32),
            pltpu.VMEM((length * groups, LANES), jnp.float32),
            pltpu.VMEM((length * groups, LANES), jnp.float32),
            pltpu.VMEM((length * groups, LANES), jnp.float32),
            pltpu.VMEM((2, modes * groups, LANES), jnp.float32),
            pltpu.VMEM((n_ctx // 2, modes * groups, LANES), jnp.float32),
            pltpu.VMEM((n_ch, length, width), jnp.bfloat16),
            pltpu.VMEM((length, features), jnp.float32),
            pltpu.SemaphoreType.DMA((6,)),
            pltpu.SemaphoreType.DMA((2,)),
            pltpu.SemaphoreType.DMA((2,)),
            pltpu.SemaphoreType.DMA((1,)),
            pltpu.SemaphoreType.DMA((1,)),
            pltpu.SemaphoreType.DMA((n_ctx,)),
            pltpu.SemaphoreType.DMA((n_ctx // 2, 2)),
            pltpu.SemaphoreType.DMA((2, n_ch, parts)),
            pltpu.SemaphoreType.DMA((n_ch, parts)),
        ],
        compiler_params=pltpu.CompilerParams(
            collective_id=0, has_side_effects=True, vmem_limit_bytes=62 * 1024 * 1024 + 640 * 1024
        ),
        cost_estimate=pl.CostEstimate(
            flops=2 * length * total_width * features,
            bytes_accessed=2 * (total_width * features + 3 * width * length + length * features),
            transcendentals=0,
        ),
    )(proj, short_filter.transpose(0, 2, 1), residues.T, decays.T, skip[None, :], w_out)


def solution(mesh):
    in_specs = (
        P(None, "ch", "ctx"),
        P(None, "ch", None),
        P("ch", None),
        P("ch", None),
        P("ch"),
        P(None, "ch"),
    )
    dims_mesh = (mesh.shape["ctx"], mesh.shape["ch"])
    return jax.shard_map(
        functools.partial(per_device, dims_mesh),
        mesh=mesh, in_specs=in_specs, out_specs=P("ctx", "ch"), check_vma=False,
    )
```

```python
import functools

import jax
import jax.numpy as jnp
from jax import lax
from jax.experimental import pallas as pl
from jax.experimental.pallas import tpu as pltpu
from jax.sharding import PartitionSpec as P

MESH = pl.DeviceIdType.MESH
LANES = 128


def rounded(value):
    return value.astype(jnp.bfloat16).astype(jnp.float32)


def fused_kernel(
    dims, proj_hbm, short_hbm, weight_hbm, rate_hbm, skip_hbm, w_hbm, out_ref,
    proj_v, short_v, weight_v, rate_v, skip_v, coef_ref, w_v, mixed, signal, query, gate_rows, pair, chips,
    gathered, total, help_v, partial,
    in_sem, halo_send, halo_recv, pair_send, pair_recv, state_send, state_recv, send_sem, recv_sem,
    piece_sem, spread_send, spread_recv, partial_send, partial_recv,
):
    n_ctx, n_ch, length, groups, modes, halo, parts, features = dims
    width = groups * LANES
    rows = length // parts
    ctx = lax.axis_index("ctx")
    ch = lax.axis_index("ch")

    small = [
        pltpu.make_async_copy(source, target, in_sem.at[2 + k])
        for k, (source, target) in enumerate(
            [(rate_hbm, rate_v), (weight_hbm, weight_v), (short_hbm, short_v), (skip_hbm, skip_v)]
        )
    ]
    for copy in small:
        copy.start()
    load_proj = pltpu.make_async_copy(proj_hbm, proj_v, in_sem.at[0])
    load_proj.start()
    load_w = pltpu.make_async_copy(w_hbm, w_v, in_sem.at[1])
    load_w.start()

    barrier = pltpu.get_barrier_semaphore()

    def greet(step, carry):
        pl.semaphore_signal(
            barrier, inc=1, device_id={"ctx": lax.rem(ctx + step, n_ctx)}, device_id_type=MESH
        )
        return carry

    lax.fori_loop(1, n_ctx, greet, 0)

    @pl.when(ch > 0)
    def _():
        pl.semaphore_signal(barrier, inc=1, device_id={"ch": ch - 1}, device_id_type=MESH)

    @pl.when(ch < n_ch - 1)
    def _():
        pl.semaphore_signal(barrier, inc=1, device_id={"ch": ch + 1}, device_id_type=MESH)

    inner = jnp.where(ch > 0, 1, 0) + jnp.where(ch < n_ch - 1, 1, 0)

    for copy in small:
        copy.wait()

    def spread(base, value):
        for group in range(groups):
            coef_ref[pl.ds(base * groups + group, value.shape[0], stride=groups), :] = (
                value[:, group * LANES:(group + 1) * LANES]
            )

    rate = rate_v[...]
    spread(0, jnp.exp(-rate))
    spread(modes, weight_v[...] * jnp.sqrt(jnp.tanh(rate) * (1.0 + jnp.exp(-2.0 * rate))))
    spread(2 * modes, jnp.exp(-float(length) * rate))
    spread(3 * modes, jnp.exp(-float(length - 2) * rate))
    for i in range(3):
        spread(4 * modes + 3 * i, short_v[i])
    spread(4 * modes + 9, skip_v[...])

    def coef(index):
        return coef_ref[index * groups:(index + 1) * groups, :]

    decay = [coef(m) for m in range(modes)]
    taps = [[coef(4 * modes + 3 * i + m) for m in range(3)] for i in range(3)]
    skip = coef(4 * modes + 9)

    load_proj.wait()
    row_ids = lax.broadcasted_iota(jnp.int32, (length, length), 0)
    col_ids = lax.broadcasted_iota(jnp.int32, (length, length), 1)
    eye = jnp.where(row_ids == col_ids, 1.0, 0.0).astype(jnp.bfloat16)
    wide = min(width, 256)

    def turn(i):
        for part in range(width // wide):
            turned = lax.dot_general(
                eye, proj_v[i, part * wide:(part + 1) * wide, :],
                (((1,), (1,)), ((), ())), preferred_element_type=jnp.float32,
            )
            for j in range(wide // LANES):
                group = part * (wide // LANES) + j
                mixed[i, pl.ds(halo * groups + group, length, stride=groups), :] = (
                    turned[:, j * LANES:(j + 1) * LANES]
                )

    turn(1)
    turn(2)

    pl.semaphore_wait(barrier, n_ctx - 1 + inner)

    helped = n_ch == 4 and n_ctx == 8
    cut = parts // 2
    at_end = (ch == 0) | (ch == n_ch - 1)
    inside = jnp.logical_not(at_end)
    piece = 2 * width // n_ctx
    far = jnp.where(ch < n_ch // 2, 2, 0)

    def piece_window(index, which):
        return pl.ds(
            pl.multiple_of(index * piece + which * (piece // 2), piece // 2), piece // 2
        )

    def piece_copy():
        return pltpu.make_async_remote_copy(
            src_ref=w_hbm.at[pl.ds(pl.multiple_of(far * width + ctx * piece, piece), piece), :],
            dst_ref=help_v.at[pl.ds(pl.multiple_of(ctx * piece, piece), piece), :],
            send_sem=piece_sem.at[0],
            recv_sem=piece_sem.at[1],
            device_id={"ch": jnp.where(ch < n_ch // 2, 1, n_ch - 2)},
            device_id_type=MESH,
        )

    def across(index):
        return index + 2 - 4 * lax.rem(index // 2, 2)

    x_peer = across(ctx)
    y_peer = ctx + 4 - 8 * (ctx // 4)
    corner = across(y_peer)
    core_peer = ctx + 1 - 2 * lax.rem(ctx, 2)
    peers = (x_peer, y_peer, core_peer)

    def spread_copy(way, index, which):
        window = help_v.at[piece_window(index, which), :]
        return pltpu.make_async_remote_copy(
            src_ref=window,
            dst_ref=window,
            send_sem=spread_send.at[way, index, which],
            recv_sem=spread_recv.at[index, which],
            device_id={"ctx": peers[way]},
            device_id_type=MESH,
        )

    spread_stages = (
        ((0, ctx, 0), (1, ctx, 1), (2, ctx, 0), (2, ctx, 1)),
        ((1, ctx, 0), (1, x_peer, 0), (0, ctx, 1), (0, y_peer, 1), (2, x_peer, 0), (2, y_peer, 1)),
        ((2, y_peer, 0), (2, corner, 0), (2, x_peer, 1), (2, corner, 1)),
    )
    spread_waits = (
        (),
        ((x_peer, 0), (y_peer, 1)),
        ((y_peer, 0), (corner, 0), (x_peer, 1), (corner, 1)),
    )

    def spread_stage(stage):
        @pl.when(inside)
        def _():
            if stage == 0:
                piece_copy().wait_recv()
            for index, which in spread_waits[stage]:
                spread_copy(0, index, which).wait_recv()
            for way, index, which in spread_stages[stage]:
                spread_copy(way, index, which).start()

    if helped:
        @pl.when(at_end)
        def _():
            piece_copy().start()

    edge = halo * groups

    def halo_copy(first, count):
        return pltpu.make_async_remote_copy(
            src_ref=mixed.at[first:first + count, pl.ds(length * groups, edge), :],
            dst_ref=mixed.at[first:first + count, pl.ds(0, edge), :],
            send_sem=halo_send.at[first],
            recv_sem=halo_recv.at[first],
            device_id={"ctx": lax.rem(ctx + 1, n_ctx)},
            device_id_type=MESH,
        )

    @pl.when(ctx < n_ctx - 1)
    def _():
        halo_copy(1, 2).start()

    @pl.when(ctx == 0)
    def _():
        mixed[:, pl.ds(0, edge), :] = jnp.zeros((3, edge, LANES), jnp.float32)

    def short(i, t):
        def at(back):
            start = (t + halo - back) * groups
            if not isinstance(start, int):
                start = pl.multiple_of(start, groups)
            return mixed[i, pl.ds(start, groups), :]

        return taps[i][0] * at(0) + taps[i][1] * at(1) + taps[i][2] * at(2)

    def row_of(t):
        start = t * groups
        if not isinstance(start, int):
            start = pl.multiple_of(start, groups)
        return pl.ds(start, groups)

    def absorb(t, state):
        value = rounded(short(1, t) * short(2, t))
        signal[row_of(t), :] = value
        return tuple(d * s + value for d, s in zip(decay, state))

    empty = tuple(jnp.zeros((groups, LANES), jnp.float32) for _ in range(modes))
    state = empty
    for t in range(2, 8):
        state = absorb(t, state)
    state = lax.fori_loop(8, length, absorb, state, unroll=8)

    @pl.when(ctx > 0)
    def _():
        halo_copy(1, 2).wait_recv()

    first = rounded(short(1, 0) * short(2, 0))
    second = rounded(short(1, 1) * short(2, 1))
    signal[row_of(0), :] = first
    signal[row_of(1), :] = second

    chip, core = ctx // 2, lax.rem(ctx, 2)
    half = modes * groups // 2
    for m in range(modes):
        own = state[m] + coef(3 * modes + m) * (decay[m] * first + second)
        pair[core, m * groups:(m + 1) * groups, :] = own

    def pair_copy(source):
        return pltpu.make_async_remote_copy(
            src_ref=pair.at[source],
            dst_ref=pair.at[source],
            send_sem=pair_send.at[0],
            recv_sem=pair_recv.at[0],
            device_id={"ctx": 2 * chip + 1 - core},
            device_id_type=MESH,
        )

    pair_copy(core).start()
    turn(0)

    @pl.when(ctx < n_ctx - 1)
    def _():
        halo_copy(0, 1).start()

    pair_copy(1 - core).wait_recv()

    def half_rows(which, base=0):
        return pl.ds(pl.multiple_of(base + which * half, half), half)

    chips[chip, half_rows(core), :] = (
        coef_ref[half_rows(core, 2 * modes * groups), :] * pair[0, half_rows(core), :]
        + pair[1, half_rows(core), :]
    )

    def chip_copy(source, which, target):
        window = chips.at[source, half_rows(which), :]
        return pltpu.make_async_remote_copy(
            src_ref=window,
            dst_ref=window,
            send_sem=state_send.at[target],
            recv_sem=state_recv.at[source, which],
            device_id={"ctx": target},
            device_id_type=MESH,
        )

    def send_chip(target, carry):
        chip_copy(chip, core, target).start()
        return carry

    lax.fori_loop(2 * chip + 2, n_ctx, send_chip, 0)

    def project(t, carry):
        query[row_of(t), :] = rounded(short(0, t))
        return carry

    for t in range(2, 8):
        project(t, 0)
    lax.fori_loop(8, length, project, 0, unroll=8)

    @pl.when(ctx > 0)
    def _():
        halo_copy(0, 1).wait_recv()

    for t in range(2):
        query[row_of(t), :] = rounded(short(0, t))

    def take_chip(source, carried):
        for which in range(2):
            chip_copy(source, which, ctx).wait_recv()
        return tuple(
            coef(2 * modes + m) * (coef(2 * modes + m) * carried[m])
            + chips[source, m * groups:(m + 1) * groups, :]
            for m in range(modes)
        )

    state = lax.fori_loop(0, chip, take_chip, empty)
    odd = core == 1
    state = tuple(
        jnp.where(
            odd,
            coef(2 * modes + m) * state[m] + pair[0, m * groups:(m + 1) * groups, :],
            state[m],
        )
        for m in range(modes)
    )
    gain = [coef(modes + m) for m in range(modes)]

    def summed(terms):
        while len(terms) > 1:
            terms = [sum(terms[k:k + 2][1:], terms[k]) for k in range(0, len(terms), 2)]
        return terms[0]

    def finish(t, state):
        value = signal[row_of(t), :]
        state = tuple(d * s + value for d, s in zip(decay, state))
        conv = rounded(summed([g * s for g, s in zip(gain, state)]))
        gate_rows[row_of(t), :] = query[row_of(t), :] * (conv + skip * value)
        return state

    def block_copy(block, part, side):
        window = gathered.at[block, pl.ds(pl.multiple_of(part * rows, rows), rows), :]
        return pltpu.make_async_remote_copy(
            src_ref=window,
            dst_ref=window,
            send_sem=send_sem.at[side, block, part],
            recv_sem=recv_sem.at[block, part],
            device_id={"ch": jnp.clip(ch - 1 + 2 * side, 0, n_ch - 1)},
            device_id_type=MESH,
        )

    for part in range(parts):
        state = lax.fori_loop(part * rows, (part + 1) * rows, finish, state, unroll=4)
        for group in range(groups):
            tile = gate_rows[pl.ds(part * rows * groups + group, rows, stride=groups), :]
            gathered[ch, part * rows:(part + 1) * rows, group * LANES:(group + 1) * LANES] = (
                tile.astype(jnp.bfloat16)
            )

        @pl.when(ch > 0)
        def _():
            block_copy(ch, part, 0).start()

        @pl.when(ch < n_ch - 1)
        def _():
            block_copy(ch, part, 1).start()

        if helped and part == 3:
            spread_stage(0)

    load_w.wait()

    slabs = min(parts, max(1, features // 256))
    slab = features // slabs

    def window(part):
        return pl.ds(pl.multiple_of(part * rows, rows), rows)

    def weight_rows(block):
        return pl.ds(pl.multiple_of(block * width, width), width)

    def add_columns(block, part, fresh, height):
        cols = pl.ds(pl.multiple_of(part * slab, slab), slab)
        value = jnp.dot(
            gathered[block, :height, :], w_v[weight_rows(block), cols],
            preferred_element_type=jnp.float32,
        )
        if fresh:
            total[:height, cols] = value
        else:
            total[:height, cols] += value

    def add_rows(block, part):
        total[window(part), :] += jnp.dot(
            gathered[block, window(part), :], w_v[weight_rows(block), :],
            preferred_element_type=jnp.float32,
        )

    def block_at(distance, side):
        if side == 0:
            return ch + distance, ch + distance < n_ch
        return ch - distance, ch >= distance

    def arriving(distance, side, part):
        block, here = block_at(distance, side)
        if helped and distance > 1:
            here = here & (inside | (part < cut))
        return block, here

    def partial_copy(piece_at):
        span = length // 4
        window_at = partial.at[piece_at * span:(piece_at + 1) * span, :]
        return pltpu.make_async_remote_copy(
            src_ref=window_at,
            dst_ref=window_at,
            send_sem=partial_send.at[piece_at],
            recv_sem=partial_recv.at[piece_at],
            device_id={"ch": jnp.where(ch < n_ch // 2, 0, n_ch - 1)},
            device_id_type=MESH,
        )

    def send_partial(piece_at):
        span = length // 4
        first = length // 2 + piece_at * span

        @pl.when(inside)
        def _():
            if piece_at == 0:
                for index in (ctx, x_peer, y_peer, corner):
                    other = index + 1 - 2 * lax.rem(index, 2)
                    for which in range(2):
                        spread_copy(2, other, which).wait_recv()
            value = jnp.dot(
                gathered[far, first:first + span, :], help_v[:width, :],
                preferred_element_type=jnp.float32,
            ) + jnp.dot(
                gathered[far + 1, first:first + span, :], help_v[width:, :],
                preferred_element_type=jnp.float32,
            )
            partial[piece_at * span:(piece_at + 1) * span, :] = value.astype(jnp.bfloat16)
            partial_copy(piece_at).start()

    for distance in range(1, n_ch):
        last = distance == n_ch - 1

        def arrive(part):
            for side in (0, 1):
                block, here = arriving(distance, side, part)
                further = (ch > 0) if side == 0 else (ch < n_ch - 1)
                if helped:
                    beyond = (ch > 1) if side == 0 else (ch < n_ch - 2)
                    further = further & (beyond | (part < cut))

                @pl.when(here)
                def _():
                    block_copy(block, part, side).wait_recv()

                @pl.when(here & further)
                def _():
                    block_copy(block, part, side).start()

        def multiply_before(part):
            if distance == 1:
                @pl.when(part < slabs)
                def _():
                    add_columns(ch, part, True, length)
                return
            for side in (0, 1):
                block, here = block_at(distance - 1, side)
                if helped and distance > 2:
                    @pl.when(here & inside & (part < slabs))
                    def _():
                        add_columns(block, part, False, length)

                    @pl.when(here & at_end & (part < slabs))
                    def _():
                        add_columns(block, part, False, length // 2)
                else:
                    @pl.when(here & (part < slabs))
                    def _():
                        add_columns(block, part, False, length)

        def multiply_rows(part):
            for side in (0, 1):
                block, here = arriving(distance, side, part)

                @pl.when(here)
                def _():
                    add_rows(block, part)

        def one_part(part, carry):
            if last and distance > 1:
                multiply_before(part)
                arrive(part)
                multiply_rows(part)
            else:
                arrive(part)
                multiply_before(part)
            return carry

        def last_rows(part, carry):
            multiply_rows(part)
            return carry

        if helped and distance == 1:
            lax.fori_loop(0, parts - 2, one_part, 0)
            spread_stage(1)
            lax.fori_loop(parts - 2, parts, one_part, 0)
        elif helped and distance == 2:
            lax.fori_loop(0, cut, one_part, 0)
            spread_stage(2)
            lax.fori_loop(cut, parts - 2, one_part, 0)
            send_partial(0)
            lax.fori_loop(parts - 2, parts, one_part, 0)
            send_partial(1)
        else:
            lax.fori_loop(0, parts, one_part, 0)
        if last and distance == 1:
            lax.fori_loop(0, parts, last_rows, 0)

    if helped:
        @pl.when(at_end)
        def _():
            span = length // 4
            for piece_at in range(2):
                partial_copy(piece_at).wait_recv()
                first = length // 2 + piece_at * span
                total[first:first + span, :] += partial[
                    piece_at * span:(piece_at + 1) * span, :
                ].astype(jnp.float32)

    out_ref[...] = total[...].astype(jnp.bfloat16)

    @pl.when(ctx < n_ctx - 1)
    def _():
        halo_copy(1, 2).wait_send()
        halo_copy(0, 1).wait_send()

    pair_copy(core).wait_send()

    def sent_chip(target, carry):
        chip_copy(chip, core, target).wait_send()
        return carry

    lax.fori_loop(2 * chip + 2, n_ctx, sent_chip, 0)

    def sent(side):
        end_next = (ch == 1) if side == 0 else (ch == n_ch - 2)

        def sent_block(block, carry):
            for part in range(parts):
                if helped and part >= cut:
                    @pl.when((block == ch) | jnp.logical_not(end_next))
                    def _():
                        block_copy(block, part, side).wait_send()
                else:
                    block_copy(block, part, side).wait_send()
            return carry

        return sent_block

    @pl.when(ch > 0)
    def _():
        lax.fori_loop(ch, n_ch, sent(0), 0)

    @pl.when(ch < n_ch - 1)
    def _():
        lax.fori_loop(0, ch + 1, sent(1), 0)

    if helped:
        @pl.when(at_end)
        def _():
            piece_copy().wait_send()

        @pl.when(inside)
        def _():
            for stage in spread_stages:
                for way, index, which in stage:
                    spread_copy(way, index, which).wait_send()
            for piece_at in range(2):
                partial_copy(piece_at).wait_send()


def per_device(dims_mesh, proj, short_filter, residues, decays, skip, w_out):
    n_ctx, n_ch = dims_mesh
    _, width, length = proj.shape
    modes = residues.shape[1]
    groups = width // LANES
    halo = max(2, 8 // groups)
    parts = 8
    features = w_out.shape[1]
    dims = (n_ctx, n_ch, length, groups, modes, halo, parts, features)
    total_width = w_out.shape[0]
    return pl.pallas_call(
        functools.partial(fused_kernel, dims),
        out_shape=jax.ShapeDtypeStruct((length, features), jnp.bfloat16),
        in_specs=[
            pl.BlockSpec(memory_space=pl.ANY),
        ] * 6,
        out_specs=pl.BlockSpec(memory_space=pltpu.VMEM),
        scratch_shapes=[
            pltpu.VMEM(proj.shape, jnp.bfloat16),
            pltpu.VMEM((3, 3, width), jnp.float32),
            pltpu.VMEM((modes, width), jnp.float32),
            pltpu.VMEM((modes, width), jnp.float32),
            pltpu.VMEM((1, width), jnp.float32),
            pltpu.VMEM(((4 * modes + 10) * groups, LANES), jnp.float32),
            pltpu.VMEM(w_out.shape, jnp.bfloat16),
            pltpu.VMEM((3, (length + halo) * groups, LANES), jnp.float32),
            pltpu.VMEM((length * groups, LANES), jnp.float32),
            pltpu.VMEM((length * groups, LANES), jnp.float32),
            pltpu.VMEM((length * groups, LANES), jnp.float32),
            pltpu.VMEM((2, modes * groups, LANES), jnp.float32),
            pltpu.VMEM((n_ctx // 2, modes * groups, LANES), jnp.float32),
            pltpu.VMEM((n_ch, length, width), jnp.bfloat16),
            pltpu.VMEM((length, features), jnp.float32),
            pltpu.VMEM((2 * width, features), jnp.bfloat16),
            pltpu.VMEM((length // 2, features), jnp.bfloat16),
            pltpu.SemaphoreType.DMA((6,)),
            pltpu.SemaphoreType.DMA((2,)),
            pltpu.SemaphoreType.DMA((2,)),
            pltpu.SemaphoreType.DMA((1,)),
            pltpu.SemaphoreType.DMA((1,)),
            pltpu.SemaphoreType.DMA((n_ctx,)),
            pltpu.SemaphoreType.DMA((n_ctx // 2, 2)),
            pltpu.SemaphoreType.DMA((2, n_ch, parts)),
            pltpu.SemaphoreType.DMA((n_ch, parts)),
            pltpu.SemaphoreType.DMA((2,)),
            pltpu.SemaphoreType.DMA((3, n_ctx, 2)),
            pltpu.SemaphoreType.DMA((n_ctx, 2)),
            pltpu.SemaphoreType.DMA((2,)),
            pltpu.SemaphoreType.DMA((2,)),
        ],
        compiler_params=pltpu.CompilerParams(
            collective_id=0, has_side_effects=True, vmem_limit_bytes=62 * 1024 * 1024 + 640 * 1024
        ),
        cost_estimate=pl.CostEstimate(
            flops=2 * length * total_width * features,
            bytes_accessed=2 * (total_width * features + 3 * width * length + length * features),
            transcendentals=0,
        ),
    )(proj, short_filter.transpose(0, 2, 1), residues.T, decays.T, skip[None, :], w_out)


def solution(mesh):
    in_specs = (
        P(None, "ch", "ctx"),
        P(None, "ch", None),
        P("ch", None),
        P("ch", None),
        P("ch"),
        P(None, "ch"),
    )
    dims_mesh = (mesh.shape["ctx"], mesh.shape["ch"])
    return jax.shard_map(
        functools.partial(per_device, dims_mesh),
        mesh=mesh, in_specs=in_specs, out_specs=P("ctx", "ch"), check_vma=False,
    )
```

```python
import functools

import jax
import jax.numpy as jnp
from jax import lax
from jax.experimental import pallas as pl
from jax.experimental.pallas import tpu as pltpu
from jax.sharding import PartitionSpec as P

MESH = pl.DeviceIdType.MESH
LANES = 128


def rounded(value):
    return value.astype(jnp.bfloat16).astype(jnp.float32)


def fused_kernel(
    dims, proj_hbm, short_hbm, weight_hbm, rate_hbm, skip_hbm, w_hbm, out_ref,
    proj_v, short_v, weight_v, rate_v, skip_v, coef_ref, w_v, mixed, signal, query, gate_rows, pair, chips,
    gathered, total, help_v, partial,
    in_sem, halo_send, halo_recv, pair_send, pair_recv, state_send, state_recv, send_sem, recv_sem,
    piece_sem, spread_send, spread_recv, partial_send, partial_recv,
):
    n_ctx, n_ch, length, groups, modes, halo, parts, features = dims
    width = groups * LANES
    rows = length // parts
    ctx = lax.axis_index("ctx")
    ch = lax.axis_index("ch")

    small = [
        pltpu.make_async_copy(source, target, in_sem.at[2 + k])
        for k, (source, target) in enumerate(
            [(rate_hbm, rate_v), (weight_hbm, weight_v), (short_hbm, short_v), (skip_hbm, skip_v)]
        )
    ]
    for copy in small:
        copy.start()
    load_proj = pltpu.make_async_copy(proj_hbm, proj_v, in_sem.at[0])
    load_proj.start()
    load_w = pltpu.make_async_copy(w_hbm, w_v, in_sem.at[1])
    load_w.start()

    barrier = pltpu.get_barrier_semaphore()

    def greet(step, carry):
        pl.semaphore_signal(
            barrier, inc=1, device_id={"ctx": lax.rem(ctx + step, n_ctx)}, device_id_type=MESH
        )
        return carry

    lax.fori_loop(1, n_ctx, greet, 0)

    @pl.when(ch > 0)
    def _():
        pl.semaphore_signal(barrier, inc=1, device_id={"ch": ch - 1}, device_id_type=MESH)

    @pl.when(ch < n_ch - 1)
    def _():
        pl.semaphore_signal(barrier, inc=1, device_id={"ch": ch + 1}, device_id_type=MESH)

    inner = jnp.where(ch > 0, 1, 0) + jnp.where(ch < n_ch - 1, 1, 0)

    for copy in small:
        copy.wait()

    def spread(base, value):
        for group in range(groups):
            coef_ref[pl.ds(base * groups + group, value.shape[0], stride=groups), :] = (
                value[:, group * LANES:(group + 1) * LANES]
            )

    rate = rate_v[...]
    spread(0, jnp.exp(-rate))
    spread(modes, weight_v[...] * jnp.sqrt(jnp.tanh(rate) * (1.0 + jnp.exp(-2.0 * rate))))
    spread(2 * modes, jnp.exp(-float(length) * rate))
    spread(3 * modes, jnp.exp(-float(length - 2) * rate))
    for i in range(3):
        spread(4 * modes + 3 * i, short_v[i])
    spread(4 * modes + 9, skip_v[...])

    def coef(index):
        return coef_ref[index * groups:(index + 1) * groups, :]

    decay = [coef(m) for m in range(modes)]
    taps = [[coef(4 * modes + 3 * i + m) for m in range(3)] for i in range(3)]
    skip = coef(4 * modes + 9)

    row_ids = lax.broadcasted_iota(jnp.int32, (length, length), 0)
    col_ids = lax.broadcasted_iota(jnp.int32, (length, length), 1)
    eye = jnp.where(row_ids == col_ids, 1.0, 0.0).astype(jnp.bfloat16)
    wide = min(width, 256)

    def turn(i):
        for part in range(width // wide):
            turned = lax.dot_general(
                eye, proj_v[i, part * wide:(part + 1) * wide, :],
                (((1,), (1,)), ((), ())), preferred_element_type=jnp.float32,
            )
            for j in range(wide // LANES):
                group = part * (wide // LANES) + j
                mixed[i, pl.ds(halo * groups + group, length, stride=groups), :] = (
                    turned[:, j * LANES:(j + 1) * LANES]
                )

    pl.semaphore_wait(barrier, n_ctx - 1 + inner)

    helped = n_ch == 4 and n_ctx == 8
    cut = parts // 2
    at_end = (ch == 0) | (ch == n_ch - 1)
    inside = jnp.logical_not(at_end)
    piece = 2 * width // n_ctx
    far = jnp.where(ch < n_ch // 2, 2, 0)

    def piece_window(index, which):
        return pl.ds(
            pl.multiple_of(index * piece + which * (piece // 2), piece // 2), piece // 2
        )

    def piece_copy(which):
        start = far * width + ctx * piece + which * (piece // 2)
        return pltpu.make_async_remote_copy(
            src_ref=w_hbm.at[pl.ds(pl.multiple_of(start, piece // 2), piece // 2), :],
            dst_ref=help_v.at[piece_window(ctx, which), :],
            send_sem=piece_sem.at[0, which],
            recv_sem=piece_sem.at[1, which],
            device_id={"ch": jnp.where(ch < n_ch // 2, 1, n_ch - 2)},
            device_id_type=MESH,
        )

    def across(index):
        return index + 2 - 4 * lax.rem(index // 2, 2)

    x_peer = across(ctx)
    y_peer = ctx + 4 - 8 * (ctx // 4)
    corner = across(y_peer)
    core_peer = ctx + 1 - 2 * lax.rem(ctx, 2)
    peers = (x_peer, y_peer, core_peer)

    def spread_copy(way, index, which):
        window = help_v.at[piece_window(index, which), :]
        return pltpu.make_async_remote_copy(
            src_ref=window,
            dst_ref=window,
            send_sem=spread_send.at[way, index, which],
            recv_sem=spread_recv.at[index, which],
            device_id={"ctx": peers[way]},
            device_id_type=MESH,
        )

    spread_stages = (
        ((0, ctx, 0), (2, ctx, 0)),
        ((1, ctx, 1), (2, ctx, 1)),
        ((1, ctx, 0), (1, x_peer, 0), (2, x_peer, 0)),
        ((0, ctx, 1), (0, y_peer, 1), (2, y_peer, 1)),
        ((2, y_peer, 0), (2, corner, 0), (2, x_peer, 1), (2, corner, 1)),
    )
    spread_waits = (
        (),
        (),
        ((x_peer, 0),),
        ((y_peer, 1),),
        ((y_peer, 0), (corner, 0), (x_peer, 1), (corner, 1)),
    )

    def spread_stage(stage):
        @pl.when(inside)
        def _():
            if stage < 2:
                piece_copy(stage).wait_recv()
            for index, which in spread_waits[stage]:
                spread_copy(0, index, which).wait_recv()
            for way, index, which in spread_stages[stage]:
                spread_copy(way, index, which).start()

    if helped:
        @pl.when(at_end)
        def _():
            for which in range(2):
                piece_copy(which).start()

    load_proj.wait()
    turn(1)
    turn(2)
    edge = halo * groups

    def halo_copy(first, count):
        return pltpu.make_async_remote_copy(
            src_ref=mixed.at[first:first + count, pl.ds(length * groups, edge), :],
            dst_ref=mixed.at[first:first + count, pl.ds(0, edge), :],
            send_sem=halo_send.at[first],
            recv_sem=halo_recv.at[first],
            device_id={"ctx": lax.rem(ctx + 1, n_ctx)},
            device_id_type=MESH,
        )

    @pl.when(ctx < n_ctx - 1)
    def _():
        halo_copy(1, 2).start()

    @pl.when(ctx == 0)
    def _():
        mixed[:, pl.ds(0, edge), :] = jnp.zeros((3, edge, LANES), jnp.float32)

    def short(i, t):
        def at(back):
            start = (t + halo - back) * groups
            if not isinstance(start, int):
                start = pl.multiple_of(start, groups)
            return mixed[i, pl.ds(start, groups), :]

        return taps[i][0] * at(0) + taps[i][1] * at(1) + taps[i][2] * at(2)

    def row_of(t):
        start = t * groups
        if not isinstance(start, int):
            start = pl.multiple_of(start, groups)
        return pl.ds(start, groups)

    def absorb(t, state):
        value = rounded(short(1, t) * short(2, t))
        signal[row_of(t), :] = value
        return tuple(d * s + value for d, s in zip(decay, state))

    empty = tuple(jnp.zeros((groups, LANES), jnp.float32) for _ in range(modes))
    state = empty
    for t in range(2, 8):
        state = absorb(t, state)
    state = lax.fori_loop(8, length, absorb, state, unroll=8)

    @pl.when(ctx > 0)
    def _():
        halo_copy(1, 2).wait_recv()

    first = rounded(short(1, 0) * short(2, 0))
    second = rounded(short(1, 1) * short(2, 1))
    signal[row_of(0), :] = first
    signal[row_of(1), :] = second

    chip, core = ctx // 2, lax.rem(ctx, 2)
    half = modes * groups // 2
    for m in range(modes):
        own = state[m] + coef(3 * modes + m) * (decay[m] * first + second)
        pair[core, m * groups:(m + 1) * groups, :] = own

    def pair_copy(source):
        return pltpu.make_async_remote_copy(
            src_ref=pair.at[source],
            dst_ref=pair.at[source],
            send_sem=pair_send.at[0],
            recv_sem=pair_recv.at[0],
            device_id={"ctx": 2 * chip + 1 - core},
            device_id_type=MESH,
        )

    pair_copy(core).start()
    turn(0)

    @pl.when(ctx < n_ctx - 1)
    def _():
        halo_copy(0, 1).start()

    pair_copy(1 - core).wait_recv()

    def half_rows(which, base=0):
        return pl.ds(pl.multiple_of(base + which * half, half), half)

    chips[chip, half_rows(core), :] = (
        coef_ref[half_rows(core, 2 * modes * groups), :] * pair[0, half_rows(core), :]
        + pair[1, half_rows(core), :]
    )

    def chip_copy(source, which, target):
        window = chips.at[source, half_rows(which), :]
        return pltpu.make_async_remote_copy(
            src_ref=window,
            dst_ref=window,
            send_sem=state_send.at[target],
            recv_sem=state_recv.at[source, which],
            device_id={"ctx": target},
            device_id_type=MESH,
        )

    def send_chip(target, carry):
        chip_copy(chip, core, target).start()
        return carry

    lax.fori_loop(2 * chip + 2, n_ctx, send_chip, 0)

    def project(t, carry):
        query[row_of(t), :] = rounded(short(0, t))
        return carry

    for t in range(2, 8):
        project(t, 0)
    lax.fori_loop(8, length, project, 0, unroll=8)

    @pl.when(ctx > 0)
    def _():
        halo_copy(0, 1).wait_recv()

    for t in range(2):
        query[row_of(t), :] = rounded(short(0, t))

    def take_chip(source, carried):
        for which in range(2):
            chip_copy(source, which, ctx).wait_recv()
        return tuple(
            coef(2 * modes + m) * (coef(2 * modes + m) * carried[m])
            + chips[source, m * groups:(m + 1) * groups, :]
            for m in range(modes)
        )

    state = lax.fori_loop(0, chip, take_chip, empty)
    odd = core == 1
    state = tuple(
        jnp.where(
            odd,
            coef(2 * modes + m) * state[m] + pair[0, m * groups:(m + 1) * groups, :],
            state[m],
        )
        for m in range(modes)
    )
    gain = [coef(modes + m) for m in range(modes)]

    def summed(terms):
        while len(terms) > 1:
            terms = [sum(terms[k:k + 2][1:], terms[k]) for k in range(0, len(terms), 2)]
        return terms[0]

    def finish(t, state):
        value = signal[row_of(t), :]
        state = tuple(d * s + value for d, s in zip(decay, state))
        conv = rounded(summed([g * s for g, s in zip(gain, state)]))
        gate_rows[row_of(t), :] = query[row_of(t), :] * (conv + skip * value)
        return state

    def block_copy(block, part, side):
        window = gathered.at[block, pl.ds(pl.multiple_of(part * rows, rows), rows), :]
        return pltpu.make_async_remote_copy(
            src_ref=window,
            dst_ref=window,
            send_sem=send_sem.at[side, block, part],
            recv_sem=recv_sem.at[block, part],
            device_id={"ch": jnp.clip(ch - 1 + 2 * side, 0, n_ch - 1)},
            device_id_type=MESH,
        )

    for part in range(parts):
        state = lax.fori_loop(part * rows, (part + 1) * rows, finish, state, unroll=4)
        for group in range(groups):
            tile = gate_rows[pl.ds(part * rows * groups + group, rows, stride=groups), :]
            gathered[ch, part * rows:(part + 1) * rows, group * LANES:(group + 1) * LANES] = (
                tile.astype(jnp.bfloat16)
            )

        @pl.when(ch > 0)
        def _():
            block_copy(ch, part, 0).start()

        @pl.when(ch < n_ch - 1)
        def _():
            block_copy(ch, part, 1).start()

        if helped and part == 0:
            spread_stage(0)
        if helped and part == 3:
            spread_stage(1)

    load_w.wait()

    slabs = min(parts, max(1, features // 256))
    slab = features // slabs

    def window(part):
        return pl.ds(pl.multiple_of(part * rows, rows), rows)

    def weight_rows(block):
        return pl.ds(pl.multiple_of(block * width, width), width)

    def add_columns(block, part, fresh, height):
        cols = pl.ds(pl.multiple_of(part * slab, slab), slab)
        value = jnp.dot(
            gathered[block, :height, :], w_v[weight_rows(block), cols],
            preferred_element_type=jnp.float32,
        )
        if fresh:
            total[:height, cols] = value
        else:
            total[:height, cols] += value

    def add_rows(block, part):
        total[window(part), :] += jnp.dot(
            gathered[block, window(part), :], w_v[weight_rows(block), :],
            preferred_element_type=jnp.float32,
        )

    def block_at(distance, side):
        if side == 0:
            return ch + distance, ch + distance < n_ch
        return ch - distance, ch >= distance

    def arriving(distance, side, part):
        block, here = block_at(distance, side)
        if helped and distance > 1:
            here = here & (inside | (part < cut))
        return block, here

    def partial_copy(piece_at):
        span = length // 4
        window_at = partial.at[piece_at * span:(piece_at + 1) * span, :]
        return pltpu.make_async_remote_copy(
            src_ref=window_at,
            dst_ref=window_at,
            send_sem=partial_send.at[piece_at],
            recv_sem=partial_recv.at[piece_at],
            device_id={"ch": jnp.where(ch < n_ch // 2, 0, n_ch - 1)},
            device_id_type=MESH,
        )

    def send_partial(piece_at):
        span = length // 4
        first = length // 2 + piece_at * span

        @pl.when(inside)
        def _():
            if piece_at == 0:
                for index in (ctx, x_peer, y_peer, corner):
                    other = index + 1 - 2 * lax.rem(index, 2)
                    for which in range(2):
                        spread_copy(2, other, which).wait_recv()
            value = jnp.dot(
                gathered[far, first:first + span, :], help_v[:width, :],
                preferred_element_type=jnp.float32,
            ) + jnp.dot(
                gathered[far + 1, first:first + span, :], help_v[width:, :],
                preferred_element_type=jnp.float32,
            )
            partial[piece_at * span:(piece_at + 1) * span, :] = value.astype(jnp.bfloat16)
            partial_copy(piece_at).start()

    for distance in range(1, n_ch):
        last = distance == n_ch - 1

        def arrive(part):
            for side in (0, 1):
                block, here = arriving(distance, side, part)
                further = (ch > 0) if side == 0 else (ch < n_ch - 1)
                if helped:
                    beyond = (ch > 1) if side == 0 else (ch < n_ch - 2)
                    further = further & (beyond | (part < cut))

                @pl.when(here)
                def _():
                    block_copy(block, part, side).wait_recv()

                @pl.when(here & further)
                def _():
                    block_copy(block, part, side).start()

        def multiply_before(part):
            if distance == 1:
                @pl.when(part < slabs)
                def _():
                    add_columns(ch, part, True, length)
                return
            for side in (0, 1):
                block, here = block_at(distance - 1, side)
                if helped and distance > 2:
                    @pl.when(here & inside & (part < slabs))
                    def _():
                        add_columns(block, part, False, length)

                    @pl.when(here & at_end & (part < slabs))
                    def _():
                        add_columns(block, part, False, length // 2)
                else:
                    @pl.when(here & (part < slabs))
                    def _():
                        add_columns(block, part, False, length)

        def multiply_rows(part):
            for side in (0, 1):
                block, here = arriving(distance, side, part)

                @pl.when(here)
                def _():
                    add_rows(block, part)

        def one_part(part, carry):
            if last and distance > 1:
                multiply_before(part)
                arrive(part)
                multiply_rows(part)
            else:
                arrive(part)
                multiply_before(part)
            return carry

        def last_rows(part, carry):
            multiply_rows(part)
            return carry

        if helped and distance == 1:
            lax.fori_loop(0, 2, one_part, 0)
            spread_stage(2)
            lax.fori_loop(2, parts - 2, one_part, 0)
            spread_stage(3)
            lax.fori_loop(parts - 2, parts, one_part, 0)
        elif helped and distance == 2:
            lax.fori_loop(0, cut, one_part, 0)
            spread_stage(4)
            lax.fori_loop(cut, parts - 2, one_part, 0)
            send_partial(0)
            lax.fori_loop(parts - 2, parts, one_part, 0)
            send_partial(1)
        else:
            lax.fori_loop(0, parts, one_part, 0)
        if last and distance == 1:
            lax.fori_loop(0, parts, last_rows, 0)

    if helped:
        @pl.when(at_end)
        def _():
            span = length // 4
            for piece_at in range(2):
                partial_copy(piece_at).wait_recv()
                first = length // 2 + piece_at * span
                total[first:first + span, :] += partial[
                    piece_at * span:(piece_at + 1) * span, :
                ].astype(jnp.float32)

    out_ref[...] = total[...].astype(jnp.bfloat16)

    @pl.when(ctx < n_ctx - 1)
    def _():
        halo_copy(1, 2).wait_send()
        halo_copy(0, 1).wait_send()

    pair_copy(core).wait_send()

    def sent_chip(target, carry):
        chip_copy(chip, core, target).wait_send()
        return carry

    lax.fori_loop(2 * chip + 2, n_ctx, sent_chip, 0)

    def sent(side):
        end_next = (ch == 1) if side == 0 else (ch == n_ch - 2)

        def sent_block(block, carry):
            for part in range(parts):
                if helped and part >= cut:
                    @pl.when((block == ch) | jnp.logical_not(end_next))
                    def _():
                        block_copy(block, part, side).wait_send()
                else:
                    block_copy(block, part, side).wait_send()
            return carry

        return sent_block

    @pl.when(ch > 0)
    def _():
        lax.fori_loop(ch, n_ch, sent(0), 0)

    @pl.when(ch < n_ch - 1)
    def _():
        lax.fori_loop(0, ch + 1, sent(1), 0)

    if helped:
        @pl.when(at_end)
        def _():
            for which in range(2):
                piece_copy(which).wait_send()

        @pl.when(inside)
        def _():
            for stage in spread_stages:
                for way, index, which in stage:
                    spread_copy(way, index, which).wait_send()
            for piece_at in range(2):
                partial_copy(piece_at).wait_send()


def per_device(dims_mesh, proj, short_filter, residues, decays, skip, w_out):
    n_ctx, n_ch = dims_mesh
    _, width, length = proj.shape
    modes = residues.shape[1]
    groups = width // LANES
    halo = max(2, 8 // groups)
    parts = 8
    features = w_out.shape[1]
    dims = (n_ctx, n_ch, length, groups, modes, halo, parts, features)
    total_width = w_out.shape[0]
    return pl.pallas_call(
        functools.partial(fused_kernel, dims),
        out_shape=jax.ShapeDtypeStruct((length, features), jnp.bfloat16),
        in_specs=[
            pl.BlockSpec(memory_space=pl.ANY),
        ] * 6,
        out_specs=pl.BlockSpec(memory_space=pltpu.VMEM),
        scratch_shapes=[
            pltpu.VMEM(proj.shape, jnp.bfloat16),
            pltpu.VMEM((3, 3, width), jnp.float32),
            pltpu.VMEM((modes, width), jnp.float32),
            pltpu.VMEM((modes, width), jnp.float32),
            pltpu.VMEM((1, width), jnp.float32),
            pltpu.VMEM(((4 * modes + 10) * groups, LANES), jnp.float32),
            pltpu.VMEM(w_out.shape, jnp.bfloat16),
            pltpu.VMEM((3, (length + halo) * groups, LANES), jnp.float32),
            pltpu.VMEM((length * groups, LANES), jnp.float32),
            pltpu.VMEM((length * groups, LANES), jnp.float32),
            pltpu.VMEM((length * groups, LANES), jnp.float32),
            pltpu.VMEM((2, modes * groups, LANES), jnp.float32),
            pltpu.VMEM((n_ctx // 2, modes * groups, LANES), jnp.float32),
            pltpu.VMEM((n_ch, length, width), jnp.bfloat16),
            pltpu.VMEM((length, features), jnp.float32),
            pltpu.VMEM((2 * width, features), jnp.bfloat16),
            pltpu.VMEM((length // 2, features), jnp.bfloat16),
            pltpu.SemaphoreType.DMA((6,)),
            pltpu.SemaphoreType.DMA((2,)),
            pltpu.SemaphoreType.DMA((2,)),
            pltpu.SemaphoreType.DMA((1,)),
            pltpu.SemaphoreType.DMA((1,)),
            pltpu.SemaphoreType.DMA((n_ctx,)),
            pltpu.SemaphoreType.DMA((n_ctx // 2, 2)),
            pltpu.SemaphoreType.DMA((2, n_ch, parts)),
            pltpu.SemaphoreType.DMA((n_ch, parts)),
            pltpu.SemaphoreType.DMA((2, 2)),
            pltpu.SemaphoreType.DMA((3, n_ctx, 2)),
            pltpu.SemaphoreType.DMA((n_ctx, 2)),
            pltpu.SemaphoreType.DMA((2,)),
            pltpu.SemaphoreType.DMA((2,)),
        ],
        compiler_params=pltpu.CompilerParams(
            collective_id=0, has_side_effects=True, vmem_limit_bytes=62 * 1024 * 1024 + 640 * 1024
        ),
        cost_estimate=pl.CostEstimate(
            flops=2 * length * total_width * features,
            bytes_accessed=2 * (total_width * features + 3 * width * length + length * features),
            transcendentals=0,
        ),
    )(proj, short_filter.transpose(0, 2, 1), residues.T, decays.T, skip[None, :], w_out)


def solution(mesh):
    in_specs = (
        P(None, "ch", "ctx"),
        P(None, "ch", None),
        P("ch", None),
        P("ch", None),
        P("ch"),
        P(None, "ch"),
    )
    dims_mesh = (mesh.shape["ctx"], mesh.shape["ch"])
    return jax.shard_map(
        functools.partial(per_device, dims_mesh),
        mesh=mesh, in_specs=in_specs, out_specs=P("ctx", "ch"), check_vma=False,
    )
```

```python
import functools

import jax
import jax.numpy as jnp
from jax import lax
from jax.experimental import pallas as pl
from jax.experimental.pallas import tpu as pltpu
from jax.sharding import PartitionSpec as P

MESH = pl.DeviceIdType.MESH
LANES = 128


def rounded(value):
    return value.astype(jnp.bfloat16).astype(jnp.float32)


def fused_kernel(
    dims, proj_hbm, short_hbm, weight_hbm, rate_hbm, skip_hbm, w_hbm, out_ref,
    proj_v, short_v, weight_v, rate_v, skip_v, coef_ref, w_v, mixed, signal, query, gate_rows, pair, chips,
    gathered, total, help_v, partial,
    in_sem, halo_send, halo_recv, pair_send, pair_recv, state_send, state_recv, send_sem, recv_sem,
    piece_sem, spread_send, spread_recv, partial_send, partial_recv,
):
    n_ctx, n_ch, length, groups, modes, halo, parts, features = dims
    width = groups * LANES
    rows = length // parts
    ctx = lax.axis_index("ctx")
    ch = lax.axis_index("ch")

    small = [
        pltpu.make_async_copy(source, target, in_sem.at[2 + k])
        for k, (source, target) in enumerate(
            [(rate_hbm, rate_v), (weight_hbm, weight_v), (short_hbm, short_v), (skip_hbm, skip_v)]
        )
    ]
    for copy in small:
        copy.start()
    load_proj = pltpu.make_async_copy(proj_hbm, proj_v, in_sem.at[0])
    load_proj.start()
    load_w = pltpu.make_async_copy(w_hbm, w_v, in_sem.at[1])
    load_w.start()

    barrier = pltpu.get_barrier_semaphore()

    def greet(step, carry):
        pl.semaphore_signal(
            barrier, inc=1, device_id={"ctx": lax.rem(ctx + step, n_ctx)}, device_id_type=MESH
        )
        return carry

    lax.fori_loop(1, n_ctx, greet, 0)

    @pl.when(ch > 0)
    def _():
        pl.semaphore_signal(barrier, inc=1, device_id={"ch": ch - 1}, device_id_type=MESH)

    @pl.when(ch < n_ch - 1)
    def _():
        pl.semaphore_signal(barrier, inc=1, device_id={"ch": ch + 1}, device_id_type=MESH)

    inner = jnp.where(ch > 0, 1, 0) + jnp.where(ch < n_ch - 1, 1, 0)

    for copy in small:
        copy.wait()

    def spread(base, value):
        for group in range(groups):
            coef_ref[pl.ds(base * groups + group, value.shape[0], stride=groups), :] = (
                value[:, group * LANES:(group + 1) * LANES]
            )

    rate = rate_v[...]
    spread(0, jnp.exp(-rate))
    spread(modes, weight_v[...] * jnp.sqrt(jnp.tanh(rate) * (1.0 + jnp.exp(-2.0 * rate))))
    spread(2 * modes, jnp.exp(-float(length) * rate))
    spread(3 * modes, jnp.exp(-float(length - 2) * rate))
    for i in range(3):
        spread(4 * modes + 3 * i, short_v[i])
    spread(4 * modes + 9, skip_v[...])

    def coef(index):
        return coef_ref[index * groups:(index + 1) * groups, :]

    decay = [coef(m) for m in range(modes)]
    taps = [[coef(4 * modes + 3 * i + m) for m in range(3)] for i in range(3)]
    skip = coef(4 * modes + 9)

    row_ids = lax.broadcasted_iota(jnp.int32, (length, length), 0)
    col_ids = lax.broadcasted_iota(jnp.int32, (length, length), 1)
    eye = jnp.where(row_ids == col_ids, 1.0, 0.0).astype(jnp.bfloat16)
    wide = min(width, 256)

    def turn(i):
        for part in range(width // wide):
            turned = lax.dot_general(
                eye, proj_v[i, part * wide:(part + 1) * wide, :],
                (((1,), (1,)), ((), ())), preferred_element_type=jnp.float32,
            )
            for j in range(wide // LANES):
                group = part * (wide // LANES) + j
                mixed[i, pl.ds(halo * groups + group, length, stride=groups), :] = (
                    turned[:, j * LANES:(j + 1) * LANES]
                )

    pl.semaphore_wait(barrier, n_ctx - 1 + inner)

    helped = n_ch == 4 and n_ctx == 8
    cut = parts // 2
    at_end = (ch == 0) | (ch == n_ch - 1)
    inside = jnp.logical_not(at_end)
    piece = 2 * width // n_ctx
    far = jnp.where(ch < n_ch // 2, 2, 0)

    def piece_window(index, which):
        return pl.ds(
            pl.multiple_of(index * piece + which * (piece // 2), piece // 2), piece // 2
        )

    def piece_copy(which):
        start = far * width + ctx * piece + which * (piece // 2)
        return pltpu.make_async_remote_copy(
            src_ref=w_hbm.at[pl.ds(pl.multiple_of(start, piece // 2), piece // 2), :],
            dst_ref=help_v.at[piece_window(ctx, which), :],
            send_sem=piece_sem.at[0, which],
            recv_sem=piece_sem.at[1, which],
            device_id={"ch": jnp.where(ch < n_ch // 2, 1, n_ch - 2)},
            device_id_type=MESH,
        )

    def across(index):
        return index + 2 - 4 * lax.rem(index // 2, 2)

    x_peer = across(ctx)
    y_peer = ctx + 4 - 8 * (ctx // 4)
    corner = across(y_peer)
    core_peer = ctx + 1 - 2 * lax.rem(ctx, 2)
    peers = (x_peer, y_peer, core_peer)

    def spread_copy(way, index, which):
        window = help_v.at[piece_window(index, which), :]
        return pltpu.make_async_remote_copy(
            src_ref=window,
            dst_ref=window,
            send_sem=spread_send.at[way, index, which],
            recv_sem=spread_recv.at[index, which],
            device_id={"ctx": peers[way]},
            device_id_type=MESH,
        )

    spread_stages = (
        ((0, ctx, 0), (2, ctx, 0)),
        ((1, ctx, 1), (2, ctx, 1)),
        ((1, ctx, 0), (1, x_peer, 0), (2, x_peer, 0)),
        ((0, ctx, 1), (0, y_peer, 1), (2, y_peer, 1)),
        ((2, y_peer, 0), (2, corner, 0), (2, x_peer, 1), (2, corner, 1)),
    )
    spread_waits = (
        (),
        (),
        ((x_peer, 0),),
        ((y_peer, 1),),
        ((y_peer, 0), (corner, 0), (x_peer, 1), (corner, 1)),
    )

    def spread_stage(stage):
        @pl.when(inside)
        def _():
            if stage < 2:
                piece_copy(stage).wait_recv()
            for index, which in spread_waits[stage]:
                spread_copy(0, index, which).wait_recv()
            for way, index, which in spread_stages[stage]:
                spread_copy(way, index, which).start()

    if helped:
        @pl.when(at_end)
        def _():
            for which in range(2):
                piece_copy(which).start()

    load_proj.wait()
    turn(1)
    turn(2)
    edge = halo * groups

    def halo_copy(first, count):
        return pltpu.make_async_remote_copy(
            src_ref=mixed.at[first:first + count, pl.ds(length * groups, edge), :],
            dst_ref=mixed.at[first:first + count, pl.ds(0, edge), :],
            send_sem=halo_send.at[first],
            recv_sem=halo_recv.at[first],
            device_id={"ctx": lax.rem(ctx + 1, n_ctx)},
            device_id_type=MESH,
        )

    @pl.when(ctx < n_ctx - 1)
    def _():
        halo_copy(1, 2).start()

    @pl.when(ctx == 0)
    def _():
        mixed[:, pl.ds(0, edge), :] = jnp.zeros((3, edge, LANES), jnp.float32)

    def short(i, t):
        def at(back):
            start = (t + halo - back) * groups
            if not isinstance(start, int):
                start = pl.multiple_of(start, groups)
            return mixed[i, pl.ds(start, groups), :]

        return taps[i][0] * at(0) + taps[i][1] * at(1) + taps[i][2] * at(2)

    def row_of(t):
        start = t * groups
        if not isinstance(start, int):
            start = pl.multiple_of(start, groups)
        return pl.ds(start, groups)

    def absorb(t, state):
        value = rounded(short(1, t) * short(2, t))
        signal[row_of(t), :] = value
        return tuple(d * s + value for d, s in zip(decay, state))

    empty = tuple(jnp.zeros((groups, LANES), jnp.float32) for _ in range(modes))
    state = empty
    for t in range(2, 8):
        state = absorb(t, state)
    state = lax.fori_loop(8, length, absorb, state, unroll=8)

    @pl.when(ctx > 0)
    def _():
        halo_copy(1, 2).wait_recv()

    first = rounded(short(1, 0) * short(2, 0))
    second = rounded(short(1, 1) * short(2, 1))
    signal[row_of(0), :] = first
    signal[row_of(1), :] = second

    chip, core = ctx // 2, lax.rem(ctx, 2)
    half = modes * groups // 2
    for m in range(modes):
        own = state[m] + coef(3 * modes + m) * (decay[m] * first + second)
        pair[core, m * groups:(m + 1) * groups, :] = own

    def pair_copy(source):
        return pltpu.make_async_remote_copy(
            src_ref=pair.at[source],
            dst_ref=pair.at[source],
            send_sem=pair_send.at[0],
            recv_sem=pair_recv.at[0],
            device_id={"ctx": 2 * chip + 1 - core},
            device_id_type=MESH,
        )

    pair_copy(core).start()
    turn(0)

    @pl.when(ctx < n_ctx - 1)
    def _():
        halo_copy(0, 1).start()

    pair_copy(1 - core).wait_recv()

    def half_rows(which, base=0):
        return pl.ds(pl.multiple_of(base + which * half, half), half)

    chips[chip, half_rows(core), :] = (
        coef_ref[half_rows(core, 2 * modes * groups), :] * pair[0, half_rows(core), :]
        + pair[1, half_rows(core), :]
    )

    def chip_copy(source, which, target):
        window = chips.at[source, half_rows(which), :]
        return pltpu.make_async_remote_copy(
            src_ref=window,
            dst_ref=window,
            send_sem=state_send.at[target],
            recv_sem=state_recv.at[source, which],
            device_id={"ctx": target},
            device_id_type=MESH,
        )

    def send_chip(target, carry):
        chip_copy(chip, core, target).start()
        return carry

    lax.fori_loop(2 * chip + 2, n_ctx, send_chip, 0)

    def project(t, carry):
        query[row_of(t), :] = rounded(short(0, t))
        return carry

    for t in range(2, 8):
        project(t, 0)
    lax.fori_loop(8, length, project, 0, unroll=8)

    @pl.when(ctx > 0)
    def _():
        halo_copy(0, 1).wait_recv()

    for t in range(2):
        query[row_of(t), :] = rounded(short(0, t))

    def take_chip(source, carried):
        for which in range(2):
            chip_copy(source, which, ctx).wait_recv()
        return tuple(
            coef(2 * modes + m) * (coef(2 * modes + m) * carried[m])
            + chips[source, m * groups:(m + 1) * groups, :]
            for m in range(modes)
        )

    if helped:
        spread_stage(0)
    state = lax.fori_loop(0, chip, take_chip, empty)
    odd = core == 1
    state = tuple(
        jnp.where(
            odd,
            coef(2 * modes + m) * state[m] + pair[0, m * groups:(m + 1) * groups, :],
            state[m],
        )
        for m in range(modes)
    )
    gain = [coef(modes + m) for m in range(modes)]

    def summed(terms):
        while len(terms) > 1:
            terms = [sum(terms[k:k + 2][1:], terms[k]) for k in range(0, len(terms), 2)]
        return terms[0]

    def finish(t, state):
        value = signal[row_of(t), :]
        state = tuple(d * s + value for d, s in zip(decay, state))
        conv = rounded(summed([g * s for g, s in zip(gain, state)]))
        gate_rows[row_of(t), :] = query[row_of(t), :] * (conv + skip * value)
        return state

    def block_copy(block, part, side):
        window = gathered.at[block, pl.ds(pl.multiple_of(part * rows, rows), rows), :]
        return pltpu.make_async_remote_copy(
            src_ref=window,
            dst_ref=window,
            send_sem=send_sem.at[side, block, part],
            recv_sem=recv_sem.at[block, part],
            device_id={"ch": jnp.clip(ch - 1 + 2 * side, 0, n_ch - 1)},
            device_id_type=MESH,
        )

    for part in range(parts):
        state = lax.fori_loop(part * rows, (part + 1) * rows, finish, state, unroll=4)
        for group in range(groups):
            tile = gate_rows[pl.ds(part * rows * groups + group, rows, stride=groups), :]
            gathered[ch, part * rows:(part + 1) * rows, group * LANES:(group + 1) * LANES] = (
                tile.astype(jnp.bfloat16)
            )

        @pl.when(ch > 0)
        def _():
            block_copy(ch, part, 0).start()

        @pl.when(ch < n_ch - 1)
        def _():
            block_copy(ch, part, 1).start()

        if helped and part == 0:
            spread_stage(1)
        if helped and part == parts - 1:
            spread_stage(2)

    load_w.wait()

    slabs = min(parts, max(1, features // 256))
    slab = features // slabs

    def window(part):
        return pl.ds(pl.multiple_of(part * rows, rows), rows)

    def weight_rows(block):
        return pl.ds(pl.multiple_of(block * width, width), width)

    def add_columns(block, part, fresh, height):
        cols = pl.ds(pl.multiple_of(part * slab, slab), slab)
        value = jnp.dot(
            gathered[block, :height, :], w_v[weight_rows(block), cols],
            preferred_element_type=jnp.float32,
        )
        if fresh:
            total[:height, cols] = value
        else:
            total[:height, cols] += value

    def add_rows(block, part):
        total[window(part), :] += jnp.dot(
            gathered[block, window(part), :], w_v[weight_rows(block), :],
            preferred_element_type=jnp.float32,
        )

    def block_at(distance, side):
        if side == 0:
            return ch + distance, ch + distance < n_ch
        return ch - distance, ch >= distance

    def arriving(distance, side, part):
        block, here = block_at(distance, side)
        if helped and distance > 1:
            here = here & (inside | (part < cut))
        return block, here

    def partial_copy(piece_at):
        span = length // 4
        window_at = partial.at[piece_at * span:(piece_at + 1) * span, :]
        return pltpu.make_async_remote_copy(
            src_ref=window_at,
            dst_ref=window_at,
            send_sem=partial_send.at[piece_at],
            recv_sem=partial_recv.at[piece_at],
            device_id={"ch": jnp.where(ch < n_ch // 2, 0, n_ch - 1)},
            device_id_type=MESH,
        )

    def send_partial(piece_at):
        span = length // 4
        first = length // 2 + piece_at * span

        @pl.when(inside)
        def _():
            if piece_at == 0:
                for index in (ctx, x_peer, y_peer, corner):
                    other = index + 1 - 2 * lax.rem(index, 2)
                    for which in range(2):
                        spread_copy(2, other, which).wait_recv()
            value = jnp.dot(
                gathered[far, first:first + span, :], help_v[:width, :],
                preferred_element_type=jnp.float32,
            ) + jnp.dot(
                gathered[far + 1, first:first + span, :], help_v[width:, :],
                preferred_element_type=jnp.float32,
            )
            partial[piece_at * span:(piece_at + 1) * span, :] = value.astype(jnp.bfloat16)
            partial_copy(piece_at).start()

    for distance in range(1, n_ch):
        last = distance == n_ch - 1

        def arrive(part):
            for side in (0, 1):
                block, here = arriving(distance, side, part)
                further = (ch > 0) if side == 0 else (ch < n_ch - 1)
                if helped:
                    beyond = (ch > 1) if side == 0 else (ch < n_ch - 2)
                    further = further & (beyond | (part < cut))

                @pl.when(here)
                def _():
                    block_copy(block, part, side).wait_recv()

                @pl.when(here & further)
                def _():
                    block_copy(block, part, side).start()

        def multiply_before(part):
            if distance == 1:
                @pl.when(part < slabs)
                def _():
                    add_columns(ch, part, True, length)
                return
            for side in (0, 1):
                block, here = block_at(distance - 1, side)
                if helped and distance > 2:
                    @pl.when(here & inside & (part < slabs))
                    def _():
                        add_columns(block, part, False, length)

                    @pl.when(here & at_end & (part < slabs))
                    def _():
                        add_columns(block, part, False, length // 2)
                else:
                    @pl.when(here & (part < slabs))
                    def _():
                        add_columns(block, part, False, length)

        def multiply_rows(part):
            for side in (0, 1):
                block, here = arriving(distance, side, part)

                @pl.when(here)
                def _():
                    add_rows(block, part)

        def one_part(part, carry):
            if last and distance > 1:
                multiply_before(part)
                arrive(part)
                multiply_rows(part)
            else:
                arrive(part)
                multiply_before(part)
            return carry

        def last_rows(part, carry):
            multiply_rows(part)
            return carry

        if helped and distance == 1:
            lax.fori_loop(0, cut, one_part, 0)
            spread_stage(3)
            lax.fori_loop(cut, parts, one_part, 0)
        elif helped and distance == 2:
            lax.fori_loop(0, cut, one_part, 0)
            spread_stage(4)
            lax.fori_loop(cut, parts - 2, one_part, 0)
            send_partial(0)
            lax.fori_loop(parts - 2, parts, one_part, 0)
            send_partial(1)
        else:
            lax.fori_loop(0, parts, one_part, 0)
        if last and distance == 1:
            lax.fori_loop(0, parts, last_rows, 0)

    if helped:
        @pl.when(at_end)
        def _():
            span = length // 4
            for piece_at in range(2):
                partial_copy(piece_at).wait_recv()
                first = length // 2 + piece_at * span
                total[first:first + span, :] += partial[
                    piece_at * span:(piece_at + 1) * span, :
                ].astype(jnp.float32)

    out_ref[...] = total[...].astype(jnp.bfloat16)

    @pl.when(ctx < n_ctx - 1)
    def _():
        halo_copy(1, 2).wait_send()
        halo_copy(0, 1).wait_send()

    pair_copy(core).wait_send()

    def sent_chip(target, carry):
        chip_copy(chip, core, target).wait_send()
        return carry

    lax.fori_loop(2 * chip + 2, n_ctx, sent_chip, 0)

    def sent(side):
        end_next = (ch == 1) if side == 0 else (ch == n_ch - 2)

        def sent_block(block, carry):
            for part in range(parts):
                if helped and part >= cut:
                    @pl.when((block == ch) | jnp.logical_not(end_next))
                    def _():
                        block_copy(block, part, side).wait_send()
                else:
                    block_copy(block, part, side).wait_send()
            return carry

        return sent_block

    @pl.when(ch > 0)
    def _():
        lax.fori_loop(ch, n_ch, sent(0), 0)

    @pl.when(ch < n_ch - 1)
    def _():
        lax.fori_loop(0, ch + 1, sent(1), 0)

    if helped:
        @pl.when(at_end)
        def _():
            for which in range(2):
                piece_copy(which).wait_send()

        @pl.when(inside)
        def _():
            for stage in spread_stages:
                for way, index, which in stage:
                    spread_copy(way, index, which).wait_send()
            for piece_at in range(2):
                partial_copy(piece_at).wait_send()


def per_device(dims_mesh, proj, short_filter, residues, decays, skip, w_out):
    n_ctx, n_ch = dims_mesh
    _, width, length = proj.shape
    modes = residues.shape[1]
    groups = width // LANES
    halo = max(2, 8 // groups)
    parts = 8
    features = w_out.shape[1]
    dims = (n_ctx, n_ch, length, groups, modes, halo, parts, features)
    total_width = w_out.shape[0]
    return pl.pallas_call(
        functools.partial(fused_kernel, dims),
        out_shape=jax.ShapeDtypeStruct((length, features), jnp.bfloat16),
        in_specs=[
            pl.BlockSpec(memory_space=pl.ANY),
        ] * 6,
        out_specs=pl.BlockSpec(memory_space=pltpu.VMEM),
        scratch_shapes=[
            pltpu.VMEM(proj.shape, jnp.bfloat16),
            pltpu.VMEM((3, 3, width), jnp.float32),
            pltpu.VMEM((modes, width), jnp.float32),
            pltpu.VMEM((modes, width), jnp.float32),
            pltpu.VMEM((1, width), jnp.float32),
            pltpu.VMEM(((4 * modes + 10) * groups, LANES), jnp.float32),
            pltpu.VMEM(w_out.shape, jnp.bfloat16),
            pltpu.VMEM((3, (length + halo) * groups, LANES), jnp.float32),
            pltpu.VMEM((length * groups, LANES), jnp.float32),
            pltpu.VMEM((length * groups, LANES), jnp.float32),
            pltpu.VMEM((length * groups, LANES), jnp.float32),
            pltpu.VMEM((2, modes * groups, LANES), jnp.float32),
            pltpu.VMEM((n_ctx // 2, modes * groups, LANES), jnp.float32),
            pltpu.VMEM((n_ch, length, width), jnp.bfloat16),
            pltpu.VMEM((length, features), jnp.float32),
            pltpu.VMEM((2 * width, features), jnp.bfloat16),
            pltpu.VMEM((length // 2, features), jnp.bfloat16),
            pltpu.SemaphoreType.DMA((6,)),
            pltpu.SemaphoreType.DMA((2,)),
            pltpu.SemaphoreType.DMA((2,)),
            pltpu.SemaphoreType.DMA((1,)),
            pltpu.SemaphoreType.DMA((1,)),
            pltpu.SemaphoreType.DMA((n_ctx,)),
            pltpu.SemaphoreType.DMA((n_ctx // 2, 2)),
            pltpu.SemaphoreType.DMA((2, n_ch, parts)),
            pltpu.SemaphoreType.DMA((n_ch, parts)),
            pltpu.SemaphoreType.DMA((2, 2)),
            pltpu.SemaphoreType.DMA((3, n_ctx, 2)),
            pltpu.SemaphoreType.DMA((n_ctx, 2)),
            pltpu.SemaphoreType.DMA((2,)),
            pltpu.SemaphoreType.DMA((2,)),
        ],
        compiler_params=pltpu.CompilerParams(
            collective_id=0, has_side_effects=True, vmem_limit_bytes=62 * 1024 * 1024 + 640 * 1024
        ),
        cost_estimate=pl.CostEstimate(
            flops=2 * length * total_width * features,
            bytes_accessed=2 * (total_width * features + 3 * width * length + length * features),
            transcendentals=0,
        ),
    )(proj, short_filter.transpose(0, 2, 1), residues.T, decays.T, skip[None, :], w_out)


def solution(mesh):
    in_specs = (
        P(None, "ch", "ctx"),
        P(None, "ch", None),
        P("ch", None),
        P("ch", None),
        P("ch"),
        P(None, "ch"),
    )
    dims_mesh = (mesh.shape["ctx"], mesh.shape["ch"])
    return jax.shard_map(
        functools.partial(per_device, dims_mesh),
        mesh=mesh, in_specs=in_specs, out_specs=P("ctx", "ch"), check_vma=False,
    )
```

```python
import functools

import jax
import jax.numpy as jnp
from jax import lax
from jax.experimental import pallas as pl
from jax.experimental.pallas import tpu as pltpu
from jax.sharding import PartitionSpec as P

MESH = pl.DeviceIdType.MESH
LANES = 128


def rounded(value):
    return value.astype(jnp.bfloat16).astype(jnp.float32)


def fused_kernel(
    dims, proj_hbm, short_hbm, weight_hbm, rate_hbm, skip_hbm, w_hbm, out_ref,
    proj_v, short_v, weight_v, rate_v, skip_v, coef_ref, w_v, mixed, signal, query, gate_rows, pair, chips,
    gathered, total,
    in_sem, halo_send, halo_recv, pair_send, pair_recv, state_send, state_recv, send_sem, recv_sem,
):
    n_ctx, n_ch, length, groups, modes, halo, parts, features = dims
    width = groups * LANES
    rows = length // parts
    ctx = lax.axis_index("ctx")
    ch = lax.axis_index("ch")

    small = [
        pltpu.make_async_copy(source, target, in_sem.at[2 + k])
        for k, (source, target) in enumerate(
            [(rate_hbm, rate_v), (weight_hbm, weight_v), (short_hbm, short_v), (skip_hbm, skip_v)]
        )
    ]
    for copy in small:
        copy.start()
    load_proj = pltpu.make_async_copy(proj_hbm, proj_v, in_sem.at[0])
    load_proj.start()
    load_w = pltpu.make_async_copy(w_hbm, w_v, in_sem.at[1])
    load_w.start()

    barrier = pltpu.get_barrier_semaphore()

    def greet(step, carry):
        pl.semaphore_signal(
            barrier, inc=1, device_id={"ctx": lax.rem(ctx + step, n_ctx)}, device_id_type=MESH
        )
        return carry

    lax.fori_loop(1, n_ctx, greet, 0)

    @pl.when(ch > 0)
    def _():
        pl.semaphore_signal(barrier, inc=1, device_id={"ch": ch - 1}, device_id_type=MESH)

    @pl.when(ch < n_ch - 1)
    def _():
        pl.semaphore_signal(barrier, inc=1, device_id={"ch": ch + 1}, device_id_type=MESH)

    inner = jnp.where(ch > 0, 1, 0) + jnp.where(ch < n_ch - 1, 1, 0)

    for copy in small:
        copy.wait()

    def spread(base, value):
        for group in range(groups):
            coef_ref[pl.ds(base * groups + group, value.shape[0], stride=groups), :] = (
                value[:, group * LANES:(group + 1) * LANES]
            )

    rate = rate_v[...]
    spread(0, jnp.exp(-rate))
    spread(modes, weight_v[...] * jnp.sqrt(jnp.tanh(rate) * (1.0 + jnp.exp(-2.0 * rate))))
    spread(2 * modes, jnp.exp(-float(length) * rate))
    spread(3 * modes, jnp.exp(-float(length - 2) * rate))
    for i in range(3):
        spread(4 * modes + 3 * i, short_v[i])
    spread(4 * modes + 9, skip_v[...])

    def coef(index):
        return coef_ref[index * groups:(index + 1) * groups, :]

    decay = [coef(m) for m in range(modes)]
    taps = [[coef(4 * modes + 3 * i + m) for m in range(3)] for i in range(3)]
    skip = coef(4 * modes + 9)

    load_proj.wait()
    row_ids = lax.broadcasted_iota(jnp.int32, (length, length), 0)
    col_ids = lax.broadcasted_iota(jnp.int32, (length, length), 1)
    eye = jnp.where(row_ids == col_ids, 1.0, 0.0).astype(jnp.bfloat16)
    wide = min(width, 256)

    def turn(i):
        for part in range(width // wide):
            turned = lax.dot_general(
                eye, proj_v[i, part * wide:(part + 1) * wide, :],
                (((1,), (1,)), ((), ())), preferred_element_type=jnp.float32,
            )
            for j in range(wide // LANES):
                group = part * (wide // LANES) + j
                mixed[i, pl.ds(halo * groups + group, length, stride=groups), :] = (
                    turned[:, j * LANES:(j + 1) * LANES]
                )

    turn(1)
    turn(2)

    pl.semaphore_wait(barrier, n_ctx - 1 + inner)

    edge = halo * groups

    def halo_copy(first, count):
        return pltpu.make_async_remote_copy(
            src_ref=mixed.at[first:first + count, pl.ds(length * groups, edge), :],
            dst_ref=mixed.at[first:first + count, pl.ds(0, edge), :],
            send_sem=halo_send.at[first],
            recv_sem=halo_recv.at[first],
            device_id={"ctx": lax.rem(ctx + 1, n_ctx)},
            device_id_type=MESH,
        )

    @pl.when(ctx < n_ctx - 1)
    def _():
        halo_copy(1, 2).start()

    @pl.when(ctx == 0)
    def _():
        mixed[:, pl.ds(0, edge), :] = jnp.zeros((3, edge, LANES), jnp.float32)

    def short(i, t):
        def at(back):
            start = (t + halo - back) * groups
            if not isinstance(start, int):
                start = pl.multiple_of(start, groups)
            return mixed[i, pl.ds(start, groups), :]

        return taps[i][0] * at(0) + taps[i][1] * at(1) + taps[i][2] * at(2)

    def row_of(t):
        start = t * groups
        if not isinstance(start, int):
            start = pl.multiple_of(start, groups)
        return pl.ds(start, groups)

    def absorb(t, state):
        value = rounded(short(1, t) * short(2, t))
        signal[row_of(t), :] = value
        return tuple(d * s + value for d, s in zip(decay, state))

    empty = tuple(jnp.zeros((groups, LANES), jnp.float32) for _ in range(modes))
    state = empty
    for t in range(2, 8):
        state = absorb(t, state)
    state = lax.fori_loop(8, length, absorb, state, unroll=8)

    @pl.when(ctx > 0)
    def _():
        halo_copy(1, 2).wait_recv()

    first = rounded(short(1, 0) * short(2, 0))
    second = rounded(short(1, 1) * short(2, 1))
    signal[row_of(0), :] = first
    signal[row_of(1), :] = second

    chip, core = ctx // 2, lax.rem(ctx, 2)
    half = modes * groups // 2
    for m in range(modes):
        own = state[m] + coef(3 * modes + m) * (decay[m] * first + second)
        pair[core, m * groups:(m + 1) * groups, :] = own

    def pair_copy(source):
        return pltpu.make_async_remote_copy(
            src_ref=pair.at[source],
            dst_ref=pair.at[source],
            send_sem=pair_send.at[0],
            recv_sem=pair_recv.at[0],
            device_id={"ctx": 2 * chip + 1 - core},
            device_id_type=MESH,
        )

    pair_copy(core).start()
    turn(0)

    @pl.when(ctx < n_ctx - 1)
    def _():
        halo_copy(0, 1).start()

    pair_copy(1 - core).wait_recv()

    def half_rows(which, base=0):
        return pl.ds(pl.multiple_of(base + which * half, half), half)

    chips[chip, half_rows(core), :] = (
        coef_ref[half_rows(core, 2 * modes * groups), :] * pair[0, half_rows(core), :]
        + pair[1, half_rows(core), :]
    )

    def chip_copy(source, which, target):
        window = chips.at[source, half_rows(which), :]
        return pltpu.make_async_remote_copy(
            src_ref=window,
            dst_ref=window,
            send_sem=state_send.at[target],
            recv_sem=state_recv.at[source, which],
            device_id={"ctx": target},
            device_id_type=MESH,
        )

    def send_chip(target, carry):
        chip_copy(chip, core, n_ctx + 2 * chip + 1 - target).start()
        return carry

    lax.fori_loop(2 * chip + 2, n_ctx, send_chip, 0)

    def project(t, carry):
        query[row_of(t), :] = rounded(short(0, t))
        return carry

    for t in range(2, 8):
        project(t, 0)
    lax.fori_loop(8, length, project, 0, unroll=8)

    @pl.when(ctx > 0)
    def _():
        halo_copy(0, 1).wait_recv()

    for t in range(2):
        query[row_of(t), :] = rounded(short(0, t))

    def take_chip(source, carried):
        for which in range(2):
            chip_copy(source, which, ctx).wait_recv()
        return tuple(
            coef(2 * modes + m) * (coef(2 * modes + m) * carried[m])
            + chips[source, m * groups:(m + 1) * groups, :]
            for m in range(modes)
        )

    state = lax.fori_loop(0, chip, take_chip, empty)
    odd = core == 1
    state = tuple(
        jnp.where(
            odd,
            coef(2 * modes + m) * state[m] + pair[0, m * groups:(m + 1) * groups, :],
            state[m],
        )
        for m in range(modes)
    )
    gain = [coef(modes + m) for m in range(modes)]

    def summed(terms):
        while len(terms) > 1:
            terms = [sum(terms[k:k + 2][1:], terms[k]) for k in range(0, len(terms), 2)]
        return terms[0]

    def finish(t, state):
        value = signal[row_of(t), :]
        state = tuple(d * s + value for d, s in zip(decay, state))
        conv = rounded(summed([g * s for g, s in zip(gain, state)]))
        gate_rows[row_of(t), :] = query[row_of(t), :] * (conv + skip * value)
        return state

    def block_copy(block, part, side):
        window = gathered.at[block, pl.ds(pl.multiple_of(part * rows, rows), rows), :]
        return pltpu.make_async_remote_copy(
            src_ref=window,
            dst_ref=window,
            send_sem=send_sem.at[side, block, part],
            recv_sem=recv_sem.at[block, part],
            device_id={"ch": jnp.clip(ch - 1 + 2 * side, 0, n_ch - 1)},
            device_id_type=MESH,
        )

    for part in range(parts):
        state = lax.fori_loop(part * rows, (part + 1) * rows, finish, state, unroll=8)
        for group in range(groups):
            tile = gate_rows[pl.ds(part * rows * groups + group, rows, stride=groups), :]
            gathered[ch, part * rows:(part + 1) * rows, group * LANES:(group + 1) * LANES] = (
                tile.astype(jnp.bfloat16)
            )

        @pl.when(ch > 0)
        def _():
            block_copy(ch, part, 0).start()

        @pl.when(ch < n_ch - 1)
        def _():
            block_copy(ch, part, 1).start()

    load_w.wait()

    slabs = min(parts, max(1, features // 256))
    slab = features // slabs

    def window(part):
        return pl.ds(pl.multiple_of(part * rows, rows), rows)

    def weight_rows(block):
        return pl.ds(pl.multiple_of(block * width, width), width)

    def add_columns(block, part, fresh):
        cols = pl.ds(pl.multiple_of(part * slab, slab), slab)
        value = jnp.dot(
            gathered[block], w_v[weight_rows(block), cols], preferred_element_type=jnp.float32
        )
        if fresh:
            total[:, cols] = value
        else:
            total[:, cols] += value

    def add_rows(block, part):
        total[window(part), :] += jnp.dot(
            gathered[block, window(part), :], w_v[weight_rows(block), :],
            preferred_element_type=jnp.float32,
        )

    def block_at(distance, side):
        if side == 0:
            return ch + distance, ch + distance < n_ch
        return ch - distance, ch >= distance

    for distance in range(1, n_ch):
        last = distance == n_ch - 1

        def arrive(part):
            for side in (0, 1):
                block, here = block_at(distance, side)
                further = (ch > 0) if side == 0 else (ch < n_ch - 1)

                @pl.when(here)
                def _():
                    block_copy(block, part, side).wait_recv()

                @pl.when(here & further)
                def _():
                    block_copy(block, part, side).start()

        def multiply_before(part):
            if distance == 1:
                @pl.when(part < slabs)
                def _():
                    add_columns(ch, part, True)
                return
            for side in (0, 1):
                block, here = block_at(distance - 1, side)

                @pl.when(here & (part < slabs))
                def _():
                    add_columns(block, part, False)

        def multiply_rows(part):
            for side in (0, 1):
                block, here = block_at(distance, side)

                @pl.when(here)
                def _():
                    add_rows(block, part)

        def one_part(part, carry):
            if last and distance > 1:
                multiply_before(part)
                arrive(part)
                multiply_rows(part)
            else:
                arrive(part)
                multiply_before(part)
            return carry

        def last_rows(part, carry):
            multiply_rows(part)
            return carry

        lax.fori_loop(0, parts, one_part, 0)
        if last and distance == 1:
            lax.fori_loop(0, parts, last_rows, 0)

    out_ref[...] = total[...].astype(jnp.bfloat16)

    @pl.when(ctx < n_ctx - 1)
    def _():
        halo_copy(1, 2).wait_send()
        halo_copy(0, 1).wait_send()

    pair_copy(core).wait_send()

    def sent_chip(target, carry):
        chip_copy(chip, core, target).wait_send()
        return carry

    lax.fori_loop(2 * chip + 2, n_ctx, sent_chip, 0)

    def sent_left(block, carry):
        for part in range(parts):
            block_copy(block, part, 0).wait_send()
        return carry

    def sent_right(block, carry):
        for part in range(parts):
            block_copy(block, part, 1).wait_send()
        return carry

    @pl.when(ch > 0)
    def _():
        lax.fori_loop(ch, n_ch, sent_left, 0)

    @pl.when(ch < n_ch - 1)
    def _():
        lax.fori_loop(0, ch + 1, sent_right, 0)


def per_device(dims_mesh, proj, short_filter, residues, decays, skip, w_out):
    n_ctx, n_ch = dims_mesh
    _, width, length = proj.shape
    modes = residues.shape[1]
    groups = width // LANES
    halo = max(2, 8 // groups)
    parts = 8
    features = w_out.shape[1]
    dims = (n_ctx, n_ch, length, groups, modes, halo, parts, features)
    total_width = w_out.shape[0]
    return pl.pallas_call(
        functools.partial(fused_kernel, dims),
        out_shape=jax.ShapeDtypeStruct((length, features), jnp.bfloat16),
        in_specs=[
            pl.BlockSpec(memory_space=pl.ANY),
        ] * 6,
        out_specs=pl.BlockSpec(memory_space=pltpu.VMEM),
        scratch_shapes=[
            pltpu.VMEM(proj.shape, jnp.bfloat16),
            pltpu.VMEM((3, 3, width), jnp.float32),
            pltpu.VMEM((modes, width), jnp.float32),
            pltpu.VMEM((modes, width), jnp.float32),
            pltpu.VMEM((1, width), jnp.float32),
            pltpu.VMEM(((4 * modes + 10) * groups, LANES), jnp.float32),
            pltpu.VMEM(w_out.shape, jnp.bfloat16),
            pltpu.VMEM((3, (length + halo) * groups, LANES), jnp.float32),
            pltpu.VMEM((length * groups, LANES), jnp.float32),
            pltpu.VMEM((length * groups, LANES), jnp.float32),
            pltpu.VMEM((length * groups, LANES), jnp.float32),
            pltpu.VMEM((2, modes * groups, LANES), jnp.float32),
            pltpu.VMEM((n_ctx // 2, modes * groups, LANES), jnp.float32),
            pltpu.VMEM((n_ch, length, width), jnp.bfloat16),
            pltpu.VMEM((length, features), jnp.float32),
            pltpu.SemaphoreType.DMA((6,)),
            pltpu.SemaphoreType.DMA((2,)),
            pltpu.SemaphoreType.DMA((2,)),
            pltpu.SemaphoreType.DMA((1,)),
            pltpu.SemaphoreType.DMA((1,)),
            pltpu.SemaphoreType.DMA((n_ctx,)),
            pltpu.SemaphoreType.DMA((n_ctx // 2, 2)),
            pltpu.SemaphoreType.DMA((2, n_ch, parts)),
            pltpu.SemaphoreType.DMA((n_ch, parts)),
        ],
        compiler_params=pltpu.CompilerParams(
            collective_id=0, has_side_effects=True, vmem_limit_bytes=62 * 1024 * 1024 + 640 * 1024
        ),
        cost_estimate=pl.CostEstimate(
            flops=2 * length * total_width * features,
            bytes_accessed=2 * (total_width * features + 3 * width * length + length * features),
            transcendentals=0,
        ),
    )(proj, short_filter.transpose(0, 2, 1), residues.T, decays.T, skip[None, :], w_out)


def solution(mesh):
    in_specs = (
        P(None, "ch", "ctx"),
        P(None, "ch", None),
        P("ch", None),
        P("ch", None),
        P("ch"),
        P(None, "ch"),
    )
    dims_mesh = (mesh.shape["ctx"], mesh.shape["ch"])
    return jax.shard_map(
        functools.partial(per_device, dims_mesh),
        mesh=mesh, in_specs=in_specs, out_specs=P("ctx", "ch"), check_vma=False,
    )
```
